32 devices in a mesh: tm: 8 (over y, x, core), seq: 4 (over z).
Axes of the slice: x: 2, y: 2, z: 4, core: 2. Of those that a mesh axis runs over, the one named last changes fastest.
Arguments:
- window_start: float32 [384, 64], P('seq'), may hold values from -6 to 6
- latents: float32 [8, 384, 64], P('tm', 'seq'), may hold values from -6 to 6
- step_index: int32 [8], P('tm'), may hold values from 0 to 63, as said below
- sigmas: float32 [65], replicated, may hold values from 0 to 1, as said below
- w_embed: bfloat16 [64, 3072], replicated, may hold values from -0.75 to 0.75
- w_mod: bfloat16 [256, 15360], P(None, 'seq'), may hold values from -0.375 to 0.375
- w_qkv: bfloat16 [3072, 6144], P(None, 'seq'), may hold values from -0.109375 to 0.109375
- qk_gain: float32 [2, 2048], P(None, 'seq'), may hold values from 0.5 to 10, as said below
- w_out: bfloat16 [2048, 3072], P(None, 'seq'), may hold values from -0.125 to 0.125
- w_final: bfloat16 [3072, 64], P('seq'), may hold values from -0.109375 to 0.109375
Outputs:
- new_latents: float32 [8, 384, 64], P('tm', 'seq')
- error: float32 [8], P('tm')
The draws below stay inside these ranges and needn't reach their ends.
Inputs may be any that keep to these rules, and one draw needn't show every extreme that they name: `step_index`: distinct and increasing along the window, the first 0 and the last 63. `sigmas`: decreasing, from 1 at entry 0 to 0 at entry 64. `qk_gain`: positive.
All inputs are finite; a program needn't handle non-finite values.
Results may differ from the reference program's by a relative error of at most 0.002.
Values may be sent and summed in bfloat16 or wider, within the bound.
A program may use at most 64 MiB of HBM per device.

```python
import math
import jax
import jax.numpy as jnp
from jax import lax

D = 3072
H = 16
HD = 128
C = 64
FREQ = 256
NSTEPS = 64
TIMESTEPS = 8
TOKENS = 384


def draw_step_index(key, part):
    key = jax.random.fold_in(key, 11)
    inner = jax.random.permutation(key, NSTEPS - 2)[:TIMESTEPS - 2].astype(jnp.int32) + 1
    first = jnp.zeros((1,), jnp.int32)
    last = jnp.full((1,), NSTEPS - 1, jnp.int32)
    chosen = jnp.concatenate([first, inner, last])
    return jnp.sort(chosen).astype(jnp.int32)


def draw_sigmas(key, part):
    key = jax.random.fold_in(key, 12)
    shift_value = jnp.exp(jax.random.uniform(key, (), jnp.float32, 0.0, math.log(7.0)))
    position = 1.0 - jnp.arange(NSTEPS + 1, dtype=jnp.float32) / NSTEPS
    return shift_value * position / (1.0 + (shift_value - 1.0) * position)


def draw_qk_gain(key, part):
    key = jax.random.fold_in(key, 13)
    first_key = jax.random.fold_in(key, 0)
    base = jnp.exp(jax.random.uniform(first_key, (2, H * HD), jnp.float32, math.log(0.5), math.log(2.0)))
    return base


def block_scale(rng, dims, cuts, least, largest):
    level = 1.0
    for axis_at, shards_of in cuts:
        heights = jax.random.uniform(jax.random.fold_in(jax.random.fold_in(rng, 6), axis_at), (shards_of,), jnp.float32, least / len(cuts), largest / len(cuts))
        level = level * jnp.repeat(jnp.exp(heights), dims[axis_at] // shards_of).reshape((-1,) + (1,) * (len(dims) - 1 - axis_at))
    return level


def noise(own_key, dims, deviation, reach, pieces=(), held_as=jnp.bfloat16):
    array = jax.random.normal(own_key, dims, jnp.float32) * deviation
    if len(pieces) > 0:
        array = block_scale(own_key, dims, pieces, -0.22, 0.18) * array
    return jnp.clip(array, min=-reach, max=reach).astype(held_as)


def setup_inputs(seed: int = 0) -> dict:
    arg_keys = jax.random.split(jax.random.key(seed), 11)
    return {
        "window_start": noise(arg_keys[0], (TOKENS, C), 1.0, 6.0, ((0, 4),), jnp.float32),
        "latents": noise(arg_keys[1], (TIMESTEPS, TOKENS, C), 1.0, 6.0, ((0, 8), (1, 4)), jnp.float32),
        "step_index": draw_step_index(jax.random.fold_in(arg_keys[10], 71), 0),
        "sigmas": draw_sigmas(jax.random.fold_in(arg_keys[10], 71), 0),
        "w_embed": noise(arg_keys[4], (C, D), C ** -0.5, 0.75),
        "w_mod": noise(arg_keys[5], (FREQ, 5 * D), FREQ ** -0.5, 0.375, ((1, 4),)),
        "w_qkv": noise(arg_keys[6], (D, 3 * H * HD), D ** -0.5, 0.109375, ((1, 4),)),
        "qk_gain": draw_qk_gain(jax.random.fold_in(arg_keys[10], 71), 0),
        "w_out": noise(arg_keys[8], (H * HD, D), (H * HD) ** -0.5, 0.125, ((1, 4),)),
        "w_final": noise(arg_keys[9], (D, C), D ** -0.5, 0.109375, ((0, 4),)),
    }


epsilon = 1e-06

def time_features(moment):
    half_width = FREQ // 2
    frequencies = jnp.exp(-math.log(10000.0) * jnp.arange(half_width, dtype=jnp.float32) / half_width)
    angles = moment * frequencies
    return jnp.concatenate([jnp.cos(angles), jnp.sin(angles)])

def layer_norm(values):
    average = lax.optimization_barrier(jnp.mean(values, axis=-1, keepdims=True))
    centered = values - average
    spread = lax.optimization_barrier(jnp.mean(centered * centered, axis=-1, keepdims=True))
    return centered * lax.rsqrt(spread + epsilon)

def rms_scale(values, gains):
    return values * lax.rsqrt(lax.optimization_barrier(jnp.mean(values * values, axis=-1, keepdims=True)) + epsilon) * gains

def drift_of(state_now, index_now, sigmas, w_embed, w_mod, w_qkv, qk_gain, w_out, w_final):
    places = jnp.arange(NSTEPS + 1, dtype=jnp.int32)
    sigma_now = jnp.sum(jnp.where(places == index_now, sigmas, jnp.zeros_like(sigmas)))
    sigma_next = jnp.sum(jnp.where(places == index_now + 1, sigmas, jnp.zeros_like(sigmas)))
    features = time_features(1000.0 * sigma_now).astype(jnp.bfloat16)[None, :]
    modulation = jnp.dot(features, w_mod, preferred_element_type=jnp.float32).reshape(5, D)
    embedded = jnp.dot(state_now.astype(jnp.bfloat16), w_embed, preferred_element_type=jnp.float32)
    shaped = (layer_norm(embedded) * (1.0 + modulation[1]) + modulation[0]).astype(jnp.bfloat16)
    mixed = jnp.dot(shaped, w_qkv, preferred_element_type=jnp.float32).reshape(TOKENS, H, 3, HD)
    gains = qk_gain.reshape(2, H, HD)
    queries = rms_scale(mixed[:, :, 0], gains[0]).astype(jnp.bfloat16)
    keys_all = rms_scale(mixed[:, :, 1], gains[1]).astype(jnp.bfloat16)
    values_all = mixed[:, :, 2].astype(jnp.bfloat16)
    scores = jnp.einsum('qhd,khd->hqk', queries.astype(jnp.float32), keys_all.astype(jnp.float32)) * HD ** (-0.5)
    weights = jax.nn.softmax(scores, axis=-1).astype(jnp.bfloat16)
    attended = jnp.einsum('hqk,khd->qhd', weights.astype(jnp.float32), values_all.astype(jnp.float32))
    attended = attended.astype(jnp.bfloat16).reshape(TOKENS, H * HD)
    hidden = embedded + modulation[2] * jnp.dot(attended, w_out, preferred_element_type=jnp.float32)
    normed = (layer_norm(hidden) * (1.0 + modulation[4]) + modulation[3]).astype(jnp.bfloat16)
    return (jnp.dot(normed, w_final, preferred_element_type=jnp.float32), sigma_next - sigma_now)

def reference(window_start, latents, step_index, sigmas, w_embed, w_mod, w_qkv, qk_gain, w_out, w_final):
    states = jnp.concatenate([window_start[None], latents[:-1]], axis=0)

    def one_step(pair):
        state_now, index_now = pair
        return drift_of(state_now, index_now, sigmas, w_embed, w_mod, w_qkv, qk_gain, w_out, w_final)
    drifts, step_sizes = lax.map(one_step, (states, step_index))
    terms = step_sizes[:, None, None] * drifts
    terms = terms.at[0].add(window_start)
    new_latents = jnp.cumsum(terms, axis=0)
    difference = new_latents - latents
    error = lax.optimization_barrier(jnp.mean(difference * difference, axis=(1, 2)))
    return (new_latents, error)
```

```python
import functools
import math

import jax
import jax.numpy as jnp
from jax import lax
from jax.experimental import pallas as pl
from jax.experimental.pallas import tpu as pltpu
from jax.sharding import PartitionSpec as P

HD = 128
FREQ = 256


epsilon = 1e-06


def shifted(x, axis, by):
    length = lax.axis_size(axis)
    pairs = [(i, i + by) for i in range(length) if 0 <= i + by < length]
    return lax.ppermute(x, axis, pairs)


def carried_in(part, axis, combine, identity):
    place = lax.axis_index(axis)
    gathered = lax.all_gather(part, axis)
    state = jnp.zeros_like(part) + jnp.asarray(identity, part.dtype)

    def one(lap, state):
        return combine(state, lax.dynamic_index_in_dim(gathered, lap, 0, False))

    return lax.fori_loop(0, place, one, state)


def time_features(moment):
    half_width = FREQ // 2
    frequencies = jnp.exp(
        -math.log(10000.0) * jnp.arange(half_width, dtype=jnp.float32) / half_width
    )
    angles = moment * frequencies
    return jnp.concatenate([jnp.cos(angles), jnp.sin(angles)])


def layer_norm(values):
    average = jnp.mean(values, axis=-1, keepdims=True)
    centered = values - average
    spread = jnp.mean(centered * centered, axis=-1, keepdims=True)
    return centered * lax.rsqrt(spread + epsilon)


def rms_scale(values, gains):
    return values * lax.rsqrt(jnp.mean(values * values, axis=-1, keepdims=True) + epsilon) * gains


def project(state_low, w_embed, modulation, w_qkv, qk_gain):
    row_total = state_low.shape[0]
    block_rows = math.gcd(row_total, 512)
    heads_here = qk_gain.shape[1] // HD
    gains = qk_gain.reshape(2, heads_here, HD)

    def project_one_block(state_block):
        embedded = jnp.dot(state_block, w_embed, preferred_element_type=jnp.float32)
        shaped = (layer_norm(embedded) * (1.0 + modulation[1]) + modulation[0]).astype(jnp.bfloat16)
        mixed = jnp.dot(shaped, w_qkv, preferred_element_type=jnp.float32).reshape(
            block_rows, heads_here, 3, HD
        )
        queries = rms_scale(mixed[:, :, 0], gains[0]).astype(jnp.bfloat16)
        keys_block = rms_scale(mixed[:, :, 1], gains[1]).astype(jnp.bfloat16)
        values_block = mixed[:, :, 2].astype(jnp.bfloat16)
        return (queries, keys_block, values_block)

    blocks = lax.map(
        project_one_block,
        state_low.reshape(row_total // block_rows, block_rows, state_low.shape[1]),
    )
    return tuple((part_block.reshape(row_total, heads_here, HD) for part_block in blocks))


def attend(queries, keys_all, values_all):
    row_total = queries.shape[0]
    heads_here = queries.shape[1]
    block_rows = math.gcd(row_total, 512)

    def attend_one_block(query_block):
        scores = jnp.einsum(
            "qhd,khd->hqk", query_block, keys_all, preferred_element_type=jnp.float32
        ) * HD ** (-0.5)
        highest = jnp.max(scores, axis=-1, keepdims=True)
        raised = jnp.exp(scores - highest)
        weights = (raised / jnp.sum(raised, axis=-1, keepdims=True)).astype(jnp.bfloat16)
        return jnp.einsum(
            "hqk,khd->qhd", weights, values_all, preferred_element_type=jnp.float32
        ).astype(jnp.bfloat16)

    blocks = lax.map(
        attend_one_block, queries.reshape(row_total // block_rows, block_rows, heads_here, HD)
    )
    return blocks.reshape(row_total, heads_here * HD)


def shards(
    window_start, latents, step_index, sigmas, w_embed, w_mod, w_qkv, qk_gain, w_out, w_final
):
    seq_count = lax.axis_size("seq")
    seq_rank = lax.axis_index("seq")
    time_rank = lax.axis_index("tm")
    tok_rows = latents.shape[1]
    all_rows = tok_rows * seq_count
    width = w_embed.shape[1]
    places = jnp.arange(sigmas.shape[0], dtype=jnp.int32)
    sigma_now = jnp.sum(jnp.where(places == step_index[0], sigmas, jnp.zeros_like(sigmas)))
    sigma_next = jnp.sum(jnp.where(places == step_index[0] + 1, sigmas, jnp.zeros_like(sigmas)))
    step_size = sigma_next - sigma_now
    features = time_features(1000.0 * sigma_now).astype(jnp.bfloat16)[None, :]
    mod_piece = jnp.dot(features, w_mod, preferred_element_type=jnp.float32)
    earlier = shifted(latents, "tm", 1)
    state_own = jnp.where(time_rank == 0, window_start, earlier[0])
    state_all, mod_rows = (
        lax.all_gather(state_own, "seq", axis=0, tiled=True),
        lax.all_gather(mod_piece, "seq", axis=0, tiled=True),
    )
    modulation = mod_rows.reshape(5, width)
    state_low = state_all.astype(jnp.bfloat16)
    queries, keys_all, values_all = project(state_low, w_embed, modulation, w_qkv, qk_gain)
    outputs = attend(queries, keys_all, values_all)
    col_count = w_out.shape[1]
    col_first = seq_rank * col_count
    own_heads = lax.all_to_all(outputs, "seq", split_axis=0, concat_axis=1, tiled=True)
    attended = jnp.dot(
        lax.all_gather(own_heads, "seq", axis=0, tiled=True),
        w_out,
        preferred_element_type=jnp.float32,
    )
    embed_cols = jnp.dot(
        state_low,
        lax.dynamic_slice_in_dim(w_embed, col_first, col_count, 1),
        preferred_element_type=jnp.float32,
    )
    mod_cols = lax.dynamic_slice_in_dim(modulation, col_first, col_count, 1)
    hidden = embed_cols + mod_cols[2] * attended
    row_sums, row_squares = lax.psum(
        (jnp.sum(hidden, axis=1), jnp.sum(hidden * hidden, axis=1)), "seq"
    )
    average = row_sums / width
    spread = row_squares / width - average * average
    centered = (hidden - average[:, None]) * lax.rsqrt(spread + epsilon)[:, None]
    normed = (centered * (1.0 + mod_cols[4]) + mod_cols[3]).astype(jnp.bfloat16)
    drift = lax.psum_scatter(
        jnp.dot(normed, w_final, preferred_element_type=jnp.float32).astype(jnp.bfloat16),
        "seq",
        scatter_dimension=0,
        tiled=True,
    ).astype(jnp.float32)
    increment = step_size * drift + jnp.where(
        time_rank == 0, window_start, jnp.zeros_like(window_start)
    )
    increment = increment[None]

    def add_terms(earlier_sum, later_sum):
        return earlier_sum + later_sum

    before = carried_in(increment, "tm", add_terms, jnp.zeros_like(increment))
    new_latents = before + increment
    difference = new_latents - latents
    total_square = lax.psum(jnp.sum(difference * difference), "seq")
    error = (total_square / (all_rows * latents.shape[2])).reshape(1)
    return (new_latents, error)


MESH = pl.DeviceIdType.MESH


def block_kernel(
    dims, index_ref, sigmas_ref, start_ref, latents_ref, gains_ref, w_embed_hbm, w_mod_hbm,
    w_qkv_hbm, w_out_hbm, w_final_hbm, new_ref, error_ref,
    w_embed, w_mod, w_qkv, w_out, w_final, state_out, state, mod, embedded, shaped, attended, total,
    part_out, parts, terms, squares,
    load_sem, qkv_sem, state_send, state_recv, mod_send, mod_recv, right_send, left_send, att_recv,
    part_send, part_recv, term_send, term_recv, square_send, square_recv,
):
    times, n, heads, rows, width, chan = dims
    cols = width // n
    all_rows = rows * n
    me_t, me = lax.axis_index("tm"), lax.axis_index("seq")
    next_t, prev_t = lax.rem(me_t + 1, times), lax.rem(me_t + times - 1, times)

    barrier = pltpu.get_barrier_semaphore()
    peers = []
    for k in range(1, n):
        other = lax.rem(me + k, n)
        peers += [(me_t, other), (next_t, other), (prev_t, other)]
    for k in range(1, times):
        peers.append((lax.rem(me_t + k, times), me))
    for peer in peers:
        pl.semaphore_signal(barrier, inc=1, device_id=peer, device_id_type=MESH)

    load_mod = pltpu.make_async_copy(w_mod_hbm, w_mod, load_sem.at[0])
    load_embed = pltpu.make_async_copy(w_embed_hbm, w_embed, load_sem.at[1])
    load_final = pltpu.make_async_copy(w_final_hbm, w_final, load_sem.at[2])
    load_out = pltpu.make_async_copy(w_out_hbm, w_out, load_sem.at[3])
    load_mod.start()
    load_embed.start()
    for h in range(heads):
        pltpu.make_async_copy(
            w_qkv_hbm.at[:, pl.ds(h * 3 * HD, 3 * HD)], w_qkv.at[h], qkv_sem.at[h]
        ).start()
    load_final.start()
    load_out.start()

    state_out[...] = jnp.where(me_t == times - 1, start_ref[...], latents_ref[0]).astype(jnp.bfloat16)

    sigma_now = sigmas_ref[index_ref[0]]
    step_size = sigmas_ref[index_ref[0] + 1] - sigma_now
    place = lax.broadcasted_iota(jnp.int32, (16, FREQ // 2), 1).astype(jnp.float32)
    angles = (1000.0 * sigma_now) * jnp.exp(place * (-math.log(10000.0) / (FREQ // 2)))
    features = jnp.concatenate([jnp.cos(angles), jnp.sin(angles)], axis=1).astype(jnp.bfloat16)

    pl.semaphore_wait(barrier, len(peers))

    def remote(source, target, send, recv, device):
        return pltpu.make_async_remote_copy(
            src_ref=source, dst_ref=target, send_sem=send, recv_sem=recv,
            device_id=device, device_id_type=MESH,
        )

    def state_copy(slot, target):
        return remote(
            state_out, state.at[slot], state_send.at[target], state_recv.at[slot], (next_t, target)
        )

    for k in range(n):
        state_copy(me, k).start()

    def mod_copy(owner, k):
        held = mod.at[pl.ds(owner * 5, 5)]
        return remote(
            held, held, mod_send.at[k], mod_recv.at[owner], (me_t, lax.rem(me + k, n))
        )

    load_mod.wait()
    for i in range(5):
        piece = jnp.dot(
            features, w_mod[:, i * cols : (i + 1) * cols], preferred_element_type=jnp.float32
        )
        mod[me * 5 + i] = piece[0:1]
    for k in range(1, n):
        mod_copy(me, k).start()

    load_embed.wait()
    for k in range(n):
        state_copy(k, 0).wait_recv()
    state_low = state[...].reshape(all_rows, chan)
    sums = jnp.zeros((all_rows, 1), jnp.float32)
    for j in range(n):
        tile = jnp.dot(
            state_low, w_embed[:, j * cols : (j + 1) * cols], preferred_element_type=jnp.float32
        )
        embedded[:, j * cols : (j + 1) * cols] = tile
        sums = sums + jnp.sum(tile, axis=1, keepdims=True)
    total[:, 0:1] = sums / width
    for k in range(1, n):
        mod_copy(lax.rem(me + k, n), k).wait_recv()

    block = 32

    def shape_rows(i, carry):
        at = pl.ds(pl.multiple_of(i * block, block), block)
        average = total[at, 0:1]
        spread = jnp.zeros((block, 1), jnp.float32)
        for j in range(n):
            centered = embedded[at, j * cols : (j + 1) * cols] - average
            spread = spread + jnp.sum(centered * centered, axis=1, keepdims=True)
        scale = lax.rsqrt(spread / width + epsilon)
        for j in range(n):
            centered = embedded[at, j * cols : (j + 1) * cols] - average
            value = centered * scale * (1.0 + mod[n + j]) + mod[j]
            shaped[at, j * cols : (j + 1) * cols] = value.astype(jnp.bfloat16)
        return carry

    lax.fori_loop(0, all_rows // block, shape_rows, 0)

    def att_copy(owner, h, right):
        slot = owner * heads + h
        sems = right_send if right else left_send
        held = attended.at[slot]
        return remote(
            held, held, sems.at[slot], att_recv.at[slot], (me_t, me + 1 if right else me - 1)
        )

    def one_head(h, carry):
        pltpu.make_async_copy(
            w_qkv_hbm.at[:, pl.ds(0, 3 * HD)], w_qkv.at[h], qkv_sem.at[h]
        ).wait()
        mixed = jnp.dot(shaped[...], w_qkv[h], preferred_element_type=jnp.float32)
        here = pl.ds(pl.multiple_of(h * HD, HD), HD)
        queries = rms_scale(mixed[:, :HD], gains_ref[0:1, here]).astype(jnp.bfloat16)
        keys = rms_scale(mixed[:, HD : 2 * HD], gains_ref[1:2, here]).astype(jnp.bfloat16)
        values = mixed[:, 2 * HD :].astype(jnp.bfloat16)
        scores = lax.dot_general(
            queries, keys, (((1,), (1,)), ((), ())), preferred_element_type=jnp.float32
        )
        raised = jnp.exp((scores - jnp.max(scores, axis=1, keepdims=True)) * HD ** (-0.5))
        weights = raised * (1.0 / jnp.sum(raised, axis=1, keepdims=True))
        attended[me * heads + h] = jnp.dot(
            weights.astype(jnp.bfloat16), values, preferred_element_type=jnp.float32
        ).astype(jnp.bfloat16)

        @pl.when(me < n - 1)
        def _():
            att_copy(me, h, True).start()

        @pl.when(me > 0)
        def _():
            att_copy(me, h, False).start()

        return carry

    lax.fori_loop(0, heads, one_head, 0)

    load_final.wait()
    load_out.wait()

    def multiply(slot):
        at = pl.ds(pl.multiple_of(slot * HD, HD), HD)
        return jnp.dot(attended[slot], w_out[at, :], preferred_element_type=jnp.float32)

    total[...] = jnp.zeros((all_rows, cols), jnp.float32)

    def own_head(h, carry):
        total[...] += multiply(me * heads + h)
        return carry

    lax.fori_loop(0, heads, own_head, 0)

    gate, shift, scale = mod[2 * n + me], mod[3 * n + me], 1.0 + mod[4 * n + me]
    final = w_final[...]
    row = lax.broadcasted_iota(jnp.int32, (16, cols), 0)

    def high(x):
        return x.astype(jnp.bfloat16).astype(jnp.float32)

    stacked = jnp.where(
        row == 0,
        high(scale),
        jnp.where(row == 1, scale - high(scale), jnp.where(row == 2, high(shift), shift - high(shift))),
    )
    sides = jnp.dot(stacked.astype(jnp.bfloat16), final, preferred_element_type=jnp.float32)
    side_row = lax.broadcasted_iota(jnp.int32, (8, chan), 0)
    sides = jnp.where(
        side_row == 0,
        sides[0:1] + sides[1:2],
        jnp.where(side_row == 1, sides[2:3] + sides[3:4], 0.0),
    )
    sides = jnp.concatenate([sides, jnp.zeros((8, 128 - chan), jnp.float32)], axis=1)

    def arrived(step, carry):
        far, h = step // heads + 1, lax.rem(step, heads)

        @pl.when(me - far >= 0)
        def _():
            att_copy(me - far, h, True).wait_recv()

            @pl.when(me < n - 1)
            def _():
                att_copy(me - far, h, True).start()

        @pl.when(me + far < n)
        def _():
            att_copy(me + far, h, False).wait_recv()

            @pl.when(me > 0)
            def _():
                att_copy(me + far, h, False).start()

        @pl.when(me - far >= 0)
        def _():
            total[...] += multiply((me - far) * heads + h)

        @pl.when(me + far < n)
        def _():
            total[...] += multiply((me + far) * heads + h)

        return carry

    lax.fori_loop(0, (n - 1) * heads, arrived, 0)

    my_cols = pl.ds(pl.multiple_of(me * cols, cols), cols)
    lane = lax.broadcasted_iota(jnp.int32, (rows, 128 - chan), 1)

    def part_of(owner):
        at = pl.ds(pl.multiple_of(owner * rows, rows), rows)
        hidden = embedded[at, my_cols] + gate * total[at, :]
        sums = jnp.sum(hidden, axis=1, keepdims=True)
        square_sums = jnp.sum(hidden * hidden, axis=1, keepdims=True)
        scaled = hidden * scale
        upper = scaled.astype(jnp.bfloat16)
        lower = (scaled - upper.astype(jnp.float32)).astype(jnp.bfloat16)
        product = jnp.dot(upper, final, preferred_element_type=jnp.float32) + jnp.dot(
            lower, final, preferred_element_type=jnp.float32
        )
        stats = jnp.where(lane == 0, sums, jnp.where(lane == 1, square_sums, 0.0))
        return jnp.concatenate([product, stats], axis=1)

    def part_copy(k, source, owner):
        return remote(
            part_out.at[k - 1], parts.at[source], part_send.at[k - 1], part_recv.at[source],
            (me_t, owner),
        )

    for k in range(1, n):
        owner = lax.rem(me + k, n)
        part_out[k - 1, :rows] = part_of(owner)
        part_out[k - 1, rows:] = sides
        part_copy(k, me, owner).start()
    parts[me, :rows] = part_of(me)
    parts[me, rows:] = sides
    for k in range(1, n):
        source = lax.rem(me + k, n)
        part_copy(k, source, source).wait_recv()
    summed = parts[0]
    for k in range(1, n):
        summed = summed + parts[k]
    average = summed[:rows, chan : chan + 1] / width
    spread = summed[:rows, chan + 1 : chan + 2] / width - average * average
    drift = (summed[:rows, :chan] - average * summed[rows : rows + 1, :chan]) * lax.rsqrt(
        spread + epsilon
    ) + summed[rows + 1 : rows + 2, :chan]
    increment = step_size * drift
    half = rows // 2
    packed = jnp.concatenate([increment[:half], increment[half:]], axis=1)
    terms[me_t] = packed

    def term_copy(source, target):
        return remote(
            terms.at[source], terms.at[source], term_send.at[target], term_recv.at[source],
            (target, me),
        )

    for k in range(1, times):

        @pl.when(me_t + k < times)
        def _():
            term_copy(me_t, me_t + k).start()

    for k in range(1, times):

        @pl.when(me_t - k >= 0)
        def _():
            term_copy(me_t - k, me_t).wait_recv()

        @pl.when(me_t - k < 0)
        def _():
            terms[me_t - k + times] = jnp.zeros((half, 128), jnp.float32)

    before = terms[0]
    for k in range(1, times):
        before = before + terms[k]
    change = jnp.concatenate([before[:, :chan], before[:, chan:]], axis=0)
    updated = start_ref[...] + change
    new_ref[0] = updated
    difference = updated - latents_ref[0]
    squares[me] = jnp.broadcast_to(jnp.sum(difference * difference), (8, 128))

    def square_copy(source, k):
        return remote(
            squares.at[source], squares.at[source], square_send.at[k], square_recv.at[source],
            (me_t, lax.rem(me + k, n)),
        )

    for k in range(1, n):
        square_copy(me, k).start()

    for k in range(n):
        state_copy(me, k).wait_send()
    for k in range(1, n):
        mod_copy(me, k).wait_send()
        part_copy(k, me, lax.rem(me + k, n)).wait_send()
    for k in range(1, times):

        @pl.when(me_t + k < times)
        def _():
            term_copy(me_t, me_t + k).wait_send()

    def all_sent(slot, carry):
        owner, h = slot // heads, lax.rem(slot, heads)

        @pl.when((owner <= me) & (me < n - 1))
        def _():
            att_copy(owner, h, True).wait_send()

        @pl.when((owner >= me) & (me > 0))
        def _():
            att_copy(owner, h, False).wait_send()

        return carry

    lax.fori_loop(0, n * heads, all_sent, 0)
    for k in range(1, n):
        square_copy(me, k).wait_send()
        square_copy(lax.rem(me + k, n), k).wait_recv()
    square_total = squares[0]
    for k in range(1, n):
        square_total = square_total + squares[k]
    error_ref[0] = jnp.max(square_total) / (all_rows * chan)


def fused(times, n, *args):
    (window_start, latents, step_index, sigmas, w_embed, w_mod, w_qkv, qk_gain, w_out, w_final) = args
    rows, chan = window_start.shape
    width = w_embed.shape[1]
    heads = qk_gain.shape[1] // HD
    cols = width // n
    low, wide = jnp.bfloat16, jnp.float32
    vmem, smem, hbm = (
        pl.BlockSpec(memory_space=space) for space in (pltpu.VMEM, pltpu.SMEM, pl.ANY)
    )
    dma = pltpu.SemaphoreType.DMA
    flops = 2 * rows * n * (width * heads * 3 * HD + n * heads * HD * cols)
    return pl.pallas_call(
        functools.partial(block_kernel, (times, n, heads, rows, width, chan)),
        out_shape=(
            jax.ShapeDtypeStruct(latents.shape, wide),
            jax.ShapeDtypeStruct((1,), wide),
        ),
        in_specs=[smem, smem, vmem, vmem, vmem, hbm, hbm, hbm, hbm, hbm],
        out_specs=(vmem, smem),
        scratch_shapes=[
            pltpu.VMEM(w_embed.shape, low),
            pltpu.VMEM(w_mod.shape, low),
            pltpu.VMEM((heads, width, 3 * HD), low),
            pltpu.VMEM(w_out.shape, low),
            pltpu.VMEM(w_final.shape, low),
            pltpu.VMEM((rows, chan), low),
            pltpu.VMEM((n, rows, chan), low),
            pltpu.VMEM((5 * n, 1, cols), wide),
            pltpu.VMEM((rows * n, width), wide),
            pltpu.VMEM((rows * n, width), low),
            pltpu.VMEM((n * heads, rows * n, HD), low),
            pltpu.VMEM((rows * n, cols), wide),
            pltpu.VMEM((n - 1, rows + 8, 128), wide),
            pltpu.VMEM((n, rows + 8, 128), wide),
            pltpu.VMEM((times, rows // 2, 128), wide),
            pltpu.VMEM((n, 8, 128), wide),
            dma((4,)),
            dma((heads,)),
            dma((n,)),
            dma((n,)),
            dma((n,)),
            dma((n,)),
            dma((n * heads,)),
            dma((n * heads,)),
            dma((n * heads,)),
            dma((n - 1,)),
            dma((n,)),
            dma((times,)),
            dma((times,)),
            dma((n,)),
            dma((n,)),
        ],
        compiler_params=pltpu.CompilerParams(
            collective_id=0, has_side_effects=True, vmem_limit_bytes=56 * 2**20
        ),
        cost_estimate=pl.CostEstimate(flops=flops, bytes_accessed=16 * 2**20, transcendentals=0),
    )(step_index, sigmas, window_start, latents, qk_gain, w_embed, w_mod, w_qkv, w_out, w_final)


def fits(times, n, args):
    rows, chan = args[0].shape
    cols = args[4].shape[1] // n
    small = rows * n * args[4].shape[1] <= 384 * 3072
    return times > 2 and n > 1 and cols % 128 == 0 and rows % 32 == 0 and chan == 64 and small


def device_part(*args):
    times, n = lax.axis_size("tm"), lax.axis_size("seq")
    if fits(times, n, args):
        return fused(times, n, *args)
    return shards(*args)


def solution(mesh):
    placed = (
        P("seq", None),
        P("tm", "seq", None),
        P("tm"),
        P(),
        P(),
        P(None, "seq"),
        P(None, "seq"),
        P(None, "seq"),
        P(None, "seq"),
        P("seq", None),
    )
    return jax.shard_map(
        device_part,
        mesh=mesh,
        in_specs=placed,
        out_specs=(P("tm", "seq", None), P("tm")),
        check_vma=False,
    )
```

```python
import functools
import math

import jax
import jax.numpy as jnp
from jax import lax
from jax.experimental import pallas as pl
from jax.experimental.pallas import tpu as pltpu
from jax.sharding import PartitionSpec as P

HD = 128
FREQ = 256


epsilon = 1e-06


def shifted(x, axis, by):
    length = lax.axis_size(axis)
    pairs = [(i, i + by) for i in range(length) if 0 <= i + by < length]
    return lax.ppermute(x, axis, pairs)


def carried_in(part, axis, combine, identity):
    place = lax.axis_index(axis)
    gathered = lax.all_gather(part, axis)
    state = jnp.zeros_like(part) + jnp.asarray(identity, part.dtype)

    def one(lap, state):
        return combine(state, lax.dynamic_index_in_dim(gathered, lap, 0, False))

    return lax.fori_loop(0, place, one, state)


def time_features(moment):
    half_width = FREQ // 2
    frequencies = jnp.exp(
        -math.log(10000.0) * jnp.arange(half_width, dtype=jnp.float32) / half_width
    )
    angles = moment * frequencies
    return jnp.concatenate([jnp.cos(angles), jnp.sin(angles)])


def layer_norm(values):
    average = jnp.mean(values, axis=-1, keepdims=True)
    centered = values - average
    spread = jnp.mean(centered * centered, axis=-1, keepdims=True)
    return centered * lax.rsqrt(spread + epsilon)


def rms_scale(values, gains):
    return values * lax.rsqrt(jnp.mean(values * values, axis=-1, keepdims=True) + epsilon) * gains


def project(state_low, w_embed, modulation, w_qkv, qk_gain):
    row_total = state_low.shape[0]
    block_rows = math.gcd(row_total, 512)
    heads_here = qk_gain.shape[1] // HD
    gains = qk_gain.reshape(2, heads_here, HD)

    def project_one_block(state_block):
        embedded = jnp.dot(state_block, w_embed, preferred_element_type=jnp.float32)
        shaped = (layer_norm(embedded) * (1.0 + modulation[1]) + modulation[0]).astype(jnp.bfloat16)
        mixed = jnp.dot(shaped, w_qkv, preferred_element_type=jnp.float32).reshape(
            block_rows, heads_here, 3, HD
        )
        queries = rms_scale(mixed[:, :, 0], gains[0]).astype(jnp.bfloat16)
        keys_block = rms_scale(mixed[:, :, 1], gains[1]).astype(jnp.bfloat16)
        values_block = mixed[:, :, 2].astype(jnp.bfloat16)
        return (queries, keys_block, values_block)

    blocks = lax.map(
        project_one_block,
        state_low.reshape(row_total // block_rows, block_rows, state_low.shape[1]),
    )
    return tuple((part_block.reshape(row_total, heads_here, HD) for part_block in blocks))


def attend(queries, keys_all, values_all):
    row_total = queries.shape[0]
    heads_here = queries.shape[1]
    block_rows = math.gcd(row_total, 512)

    def attend_one_block(query_block):
        scores = jnp.einsum(
            "qhd,khd->hqk", query_block, keys_all, preferred_element_type=jnp.float32
        ) * HD ** (-0.5)
        highest = jnp.max(scores, axis=-1, keepdims=True)
        raised = jnp.exp(scores - highest)
        weights = (raised / jnp.sum(raised, axis=-1, keepdims=True)).astype(jnp.bfloat16)
        return jnp.einsum(
            "hqk,khd->qhd", weights, values_all, preferred_element_type=jnp.float32
        ).astype(jnp.bfloat16)

    blocks = lax.map(
        attend_one_block, queries.reshape(row_total // block_rows, block_rows, heads_here, HD)
    )
    return blocks.reshape(row_total, heads_here * HD)


def shards(
    window_start, latents, step_index, sigmas, w_embed, w_mod, w_qkv, qk_gain, w_out, w_final
):
    seq_count = lax.axis_size("seq")
    seq_rank = lax.axis_index("seq")
    time_rank = lax.axis_index("tm")
    tok_rows = latents.shape[1]
    all_rows = tok_rows * seq_count
    width = w_embed.shape[1]
    places = jnp.arange(sigmas.shape[0], dtype=jnp.int32)
    sigma_now = jnp.sum(jnp.where(places == step_index[0], sigmas, jnp.zeros_like(sigmas)))
    sigma_next = jnp.sum(jnp.where(places == step_index[0] + 1, sigmas, jnp.zeros_like(sigmas)))
    step_size = sigma_next - sigma_now
    features = time_features(1000.0 * sigma_now).astype(jnp.bfloat16)[None, :]
    mod_piece = jnp.dot(features, w_mod, preferred_element_type=jnp.float32)
    earlier = shifted(latents, "tm", 1)
    state_own = jnp.where(time_rank == 0, window_start, earlier[0])
    state_all, mod_rows = (
        lax.all_gather(state_own, "seq", axis=0, tiled=True),
        lax.all_gather(mod_piece, "seq", axis=0, tiled=True),
    )
    modulation = mod_rows.reshape(5, width)
    state_low = state_all.astype(jnp.bfloat16)
    queries, keys_all, values_all = project(state_low, w_embed, modulation, w_qkv, qk_gain)
    outputs = attend(queries, keys_all, values_all)
    col_count = w_out.shape[1]
    col_first = seq_rank * col_count
    own_heads = lax.all_to_all(outputs, "seq", split_axis=0, concat_axis=1, tiled=True)
    attended = jnp.dot(
        lax.all_gather(own_heads, "seq", axis=0, tiled=True),
        w_out,
        preferred_element_type=jnp.float32,
    )
    embed_cols = jnp.dot(
        state_low,
        lax.dynamic_slice_in_dim(w_embed, col_first, col_count, 1),
        preferred_element_type=jnp.float32,
    )
    mod_cols = lax.dynamic_slice_in_dim(modulation, col_first, col_count, 1)
    hidden = embed_cols + mod_cols[2] * attended
    row_sums, row_squares = lax.psum(
        (jnp.sum(hidden, axis=1), jnp.sum(hidden * hidden, axis=1)), "seq"
    )
    average = row_sums / width
    spread = row_squares / width - average * average
    centered = (hidden - average[:, None]) * lax.rsqrt(spread + epsilon)[:, None]
    normed = (centered * (1.0 + mod_cols[4]) + mod_cols[3]).astype(jnp.bfloat16)
    drift = lax.psum_scatter(
        jnp.dot(normed, w_final, preferred_element_type=jnp.float32).astype(jnp.bfloat16),
        "seq",
        scatter_dimension=0,
        tiled=True,
    ).astype(jnp.float32)
    increment = step_size * drift + jnp.where(
        time_rank == 0, window_start, jnp.zeros_like(window_start)
    )
    increment = increment[None]

    def add_terms(earlier_sum, later_sum):
        return earlier_sum + later_sum

    before = carried_in(increment, "tm", add_terms, jnp.zeros_like(increment))
    new_latents = before + increment
    difference = new_latents - latents
    total_square = lax.psum(jnp.sum(difference * difference), "seq")
    error = (total_square / (all_rows * latents.shape[2])).reshape(1)
    return (new_latents, error)


MESH = pl.DeviceIdType.MESH


def block_kernel(
    dims, index_ref, sigmas_ref, start_ref, latents_ref, gains_ref, w_embed_hbm, w_mod_hbm,
    w_qkv_hbm, w_out_hbm, w_final_hbm, new_ref, error_ref,
    w_embed, w_mod, w_qkv, w_out, w_final, state_out, state, mod, embedded, shaped, attended, total,
    part_out, parts, terms, squares,
    load_sem, qkv_sem, state_send, state_recv, mod_send, mod_recv, right_send, left_send, att_recv,
    part_send, part_recv, term_send, term_recv, square_send, square_recv,
):
    times, n, heads, rows, width, chan = dims
    cols = width // n
    all_rows = rows * n
    me_t, me = lax.axis_index("tm"), lax.axis_index("seq")
    next_t, prev_t = lax.rem(me_t + 1, times), lax.rem(me_t + times - 1, times)

    barrier = pltpu.get_barrier_semaphore()
    peers = []
    for k in range(1, n):
        other = lax.rem(me + k, n)
        peers += [(me_t, other), (next_t, other), (prev_t, other)]
    for k in range(1, times):
        peers.append((lax.rem(me_t + k, times), me))
    for peer in peers:
        pl.semaphore_signal(barrier, inc=1, device_id=peer, device_id_type=MESH)

    load_mod = pltpu.make_async_copy(w_mod_hbm, w_mod, load_sem.at[0])
    load_embed = pltpu.make_async_copy(w_embed_hbm, w_embed, load_sem.at[1])
    load_final = pltpu.make_async_copy(w_final_hbm, w_final, load_sem.at[2])
    load_out = pltpu.make_async_copy(w_out_hbm, w_out, load_sem.at[3])
    load_mod.start()
    load_embed.start()
    for h in range(heads):
        pltpu.make_async_copy(
            w_qkv_hbm.at[:, pl.ds(h * 3 * HD, 3 * HD)], w_qkv.at[h], qkv_sem.at[h]
        ).start()
    load_final.start()
    load_out.start()

    state_out[...] = jnp.where(me_t == times - 1, start_ref[...], latents_ref[0]).T.astype(jnp.bfloat16)

    sigma_now = sigmas_ref[index_ref[0]]
    step_size = sigmas_ref[index_ref[0] + 1] - sigma_now
    place = lax.broadcasted_iota(jnp.int32, (16, FREQ // 2), 1).astype(jnp.float32)
    angles = (1000.0 * sigma_now) * jnp.exp(place * (-math.log(10000.0) / (FREQ // 2)))
    features = jnp.concatenate([jnp.cos(angles), jnp.sin(angles)], axis=1).astype(jnp.bfloat16)

    pl.semaphore_wait(barrier, len(peers))

    def remote(source, target, send, recv, device):
        return pltpu.make_async_remote_copy(
            src_ref=source, dst_ref=target, send_sem=send, recv_sem=recv,
            device_id=device, device_id_type=MESH,
        )

    def state_copy(slot, target):
        return remote(
            state_out, state.at[slot], state_send.at[target], state_recv.at[slot], (next_t, target)
        )

    for k in range(n):
        state_copy(me, k).start()

    def mod_copy(owner, k):
        held = mod.at[pl.ds(owner * 5, 5)]
        return remote(
            held, held, mod_send.at[k], mod_recv.at[owner], (me_t, lax.rem(me + k, n))
        )

    load_mod.wait()
    for i in range(5):
        piece = jnp.dot(
            features, w_mod[:, i * cols : (i + 1) * cols], preferred_element_type=jnp.float32
        )
        mod[me * 5 + i] = piece[0:1]
    for k in range(1, n):
        mod_copy(me, k).start()

    load_embed.wait()
    for k in range(n):
        state_copy(k, 0).wait_recv()
    state_low = state[...].reshape(all_rows, chan)
    sums = jnp.zeros((all_rows, 1), jnp.float32)
    for j in range(n):
        tile = jnp.dot(
            state_low, w_embed[:, j * cols : (j + 1) * cols], preferred_element_type=jnp.float32
        )
        embedded[:, j * cols : (j + 1) * cols] = tile
        sums = sums + jnp.sum(tile, axis=1, keepdims=True)
    total[:, 0:1] = sums / width
    for k in range(1, n):
        mod_copy(lax.rem(me + k, n), k).wait_recv()

    block = 32

    def shape_rows(i, carry):
        at = pl.ds(pl.multiple_of(i * block, block), block)
        average = total[at, 0:1]
        spread = jnp.zeros((block, 1), jnp.float32)
        for j in range(n):
            centered = embedded[at, j * cols : (j + 1) * cols] - average
            spread = spread + jnp.sum(centered * centered, axis=1, keepdims=True)
        scale = lax.rsqrt(spread / width + epsilon)
        for j in range(n):
            centered = embedded[at, j * cols : (j + 1) * cols] - average
            value = centered * scale * (1.0 + mod[n + j]) + mod[j]
            shaped[at, j * cols : (j + 1) * cols] = value.astype(jnp.bfloat16)
        return carry

    lax.fori_loop(0, all_rows // block, shape_rows, 0)

    def att_copy(owner, h, right):
        slot = owner * heads + h
        sems = right_send if right else left_send
        held = attended.at[slot]
        return remote(
            held, held, sems.at[slot], att_recv.at[slot], (me_t, me + 1 if right else me - 1)
        )

    def one_head(h, carry):
        pltpu.make_async_copy(
            w_qkv_hbm.at[:, pl.ds(0, 3 * HD)], w_qkv.at[h], qkv_sem.at[h]
        ).wait()
        mixed = jnp.dot(shaped[...], w_qkv[h], preferred_element_type=jnp.float32)
        here = pl.ds(pl.multiple_of(h * HD, HD), HD)
        queries = rms_scale(mixed[:, :HD], gains_ref[0:1, here]).astype(jnp.bfloat16)
        keys = rms_scale(mixed[:, HD : 2 * HD], gains_ref[1:2, here]).astype(jnp.bfloat16)
        values = mixed[:, 2 * HD :].astype(jnp.bfloat16)
        scores = lax.dot_general(
            queries, keys, (((1,), (1,)), ((), ())), preferred_element_type=jnp.float32
        )
        raised = jnp.exp((scores - jnp.max(scores, axis=1, keepdims=True)) * HD ** (-0.5))
        weights = raised * (1.0 / jnp.sum(raised, axis=1, keepdims=True))
        attended[me * heads + h] = jnp.dot(
            weights.astype(jnp.bfloat16), values, preferred_element_type=jnp.float32
        ).astype(jnp.bfloat16)

        @pl.when(me < n - 1)
        def _():
            att_copy(me, h, True).start()

        @pl.when(me > 0)
        def _():
            att_copy(me, h, False).start()

        return carry

    lax.fori_loop(0, heads, one_head, 0)

    load_final.wait()
    load_out.wait()

    def multiply(slot):
        at = pl.ds(pl.multiple_of(slot * HD, HD), HD)
        return jnp.dot(attended[slot], w_out[at, :], preferred_element_type=jnp.float32)

    total[...] = jnp.zeros((all_rows, cols), jnp.float32)

    def own_head(h, carry):
        total[...] += multiply(me * heads + h)
        return carry

    lax.fori_loop(0, heads, own_head, 0)

    gate, shift, scale = mod[2 * n + me], mod[3 * n + me], 1.0 + mod[4 * n + me]
    final = w_final[...]

    def onto_final(x):
        return lax.dot_general(x, final, (((1,), (1,)), ((), ())), preferred_element_type=jnp.float32)

    row = lax.broadcasted_iota(jnp.int32, (16, cols), 0)

    def high(x):
        return x.astype(jnp.bfloat16).astype(jnp.float32)

    stacked = jnp.where(
        row == 0,
        high(scale),
        jnp.where(row == 1, scale - high(scale), jnp.where(row == 2, high(shift), shift - high(shift))),
    )
    sides = onto_final(stacked.astype(jnp.bfloat16))
    side_row = lax.broadcasted_iota(jnp.int32, (8, chan), 0)
    sides = jnp.where(
        side_row == 0,
        sides[0:1] + sides[1:2],
        jnp.where(side_row == 1, sides[2:3] + sides[3:4], 0.0),
    )
    sides = jnp.concatenate([sides, jnp.zeros((8, 128 - chan), jnp.float32)], axis=1)

    def arrived(step, carry):
        far, h = step // heads + 1, lax.rem(step, heads)

        @pl.when(me - far >= 0)
        def _():
            att_copy(me - far, h, True).wait_recv()

            @pl.when(me < n - 1)
            def _():
                att_copy(me - far, h, True).start()

        @pl.when(me + far < n)
        def _():
            att_copy(me + far, h, False).wait_recv()

            @pl.when(me > 0)
            def _():
                att_copy(me + far, h, False).start()

        @pl.when(me - far >= 0)
        def _():
            total[...] += multiply((me - far) * heads + h)

        @pl.when(me + far < n)
        def _():
            total[...] += multiply((me + far) * heads + h)

        return carry

    lax.fori_loop(0, (n - 1) * heads, arrived, 0)

    my_cols = pl.ds(pl.multiple_of(me * cols, cols), cols)
    lane = lax.broadcasted_iota(jnp.int32, (rows, 128 - chan), 1)

    def part_of(owner):
        at = pl.ds(pl.multiple_of(owner * rows, rows), rows)
        hidden = embedded[at, my_cols] + gate * total[at, :]
        sums = jnp.sum(hidden, axis=1, keepdims=True)
        square_sums = jnp.sum(hidden * hidden, axis=1, keepdims=True)
        scaled = hidden * scale
        upper = scaled.astype(jnp.bfloat16)
        lower = (scaled - upper.astype(jnp.float32)).astype(jnp.bfloat16)
        product = onto_final(upper) + onto_final(lower)
        stats = jnp.where(lane == 0, sums, jnp.where(lane == 1, square_sums, 0.0))
        return jnp.concatenate([product, stats], axis=1)

    def part_copy(k, source, owner):
        return remote(
            part_out.at[k - 1], parts.at[source], part_send.at[k - 1], part_recv.at[source],
            (me_t, owner),
        )

    for k in range(1, n):
        owner = lax.rem(me + k, n)
        part_out[k - 1, :rows] = part_of(owner)
        part_out[k - 1, rows:] = sides
        part_copy(k, me, owner).start()
    parts[me, :rows] = part_of(me)
    parts[me, rows:] = sides
    for k in range(1, n):
        source = lax.rem(me + k, n)
        part_copy(k, source, source).wait_recv()
    summed = parts[0]
    for k in range(1, n):
        summed = summed + parts[k]
    average = summed[:rows, chan : chan + 1] / width
    spread = summed[:rows, chan + 1 : chan + 2] / width - average * average
    drift = (summed[:rows, :chan] - average * summed[rows : rows + 1, :chan]) * lax.rsqrt(
        spread + epsilon
    ) + summed[rows + 1 : rows + 2, :chan]
    increment = step_size * drift
    half = rows // 2
    packed = jnp.concatenate([increment[:half], increment[half:]], axis=1)
    terms[me_t] = packed

    def term_copy(source, target):
        return remote(
            terms.at[source], terms.at[source], term_send.at[target], term_recv.at[source],
            (target, me),
        )

    for k in range(1, times):

        @pl.when(me_t + k < times)
        def _():
            term_copy(me_t, me_t + k).start()

    for k in range(1, times):

        @pl.when(me_t - k >= 0)
        def _():
            term_copy(me_t - k, me_t).wait_recv()

        @pl.when(me_t - k < 0)
        def _():
            terms[me_t - k + times] = jnp.zeros((half, 128), jnp.float32)

    before = terms[0]
    for k in range(1, times):
        before = before + terms[k]
    change = jnp.concatenate([before[:, :chan], before[:, chan:]], axis=0)
    updated = start_ref[...] + change.T
    new_ref[0] = updated
    difference = updated - latents_ref[0]
    squares[me] = jnp.broadcast_to(jnp.sum(difference * difference), (8, 128))

    def square_copy(source, k):
        return remote(
            squares.at[source], squares.at[source], square_send.at[k], square_recv.at[source],
            (me_t, lax.rem(me + k, n)),
        )

    for k in range(1, n):
        square_copy(me, k).start()

    for k in range(n):
        state_copy(me, k).wait_send()
    for k in range(1, n):
        mod_copy(me, k).wait_send()
        part_copy(k, me, lax.rem(me + k, n)).wait_send()
    for k in range(1, times):

        @pl.when(me_t + k < times)
        def _():
            term_copy(me_t, me_t + k).wait_send()

    def all_sent(slot, carry):
        owner, h = slot // heads, lax.rem(slot, heads)

        @pl.when((owner <= me) & (me < n - 1))
        def _():
            att_copy(owner, h, True).wait_send()

        @pl.when((owner >= me) & (me > 0))
        def _():
            att_copy(owner, h, False).wait_send()

        return carry

    lax.fori_loop(0, n * heads, all_sent, 0)
    for k in range(1, n):
        square_copy(me, k).wait_send()
        square_copy(lax.rem(me + k, n), k).wait_recv()
    square_total = squares[0]
    for k in range(1, n):
        square_total = square_total + squares[k]
    error_ref[0] = jnp.max(square_total) / (all_rows * chan)


def fused(times, n, *args):
    (window_start, latents, step_index, sigmas, w_embed, w_mod, w_qkv, qk_gain, w_out, w_final) = args
    rows, chan = window_start.shape
    width = w_embed.shape[1]
    heads = qk_gain.shape[1] // HD
    cols = width // n
    low, wide = jnp.bfloat16, jnp.float32
    vmem, smem, hbm = (
        pl.BlockSpec(memory_space=space) for space in (pltpu.VMEM, pltpu.SMEM, pl.ANY)
    )
    dma = pltpu.SemaphoreType.DMA
    flops = 2 * rows * n * (width * heads * 3 * HD + n * heads * HD * cols)
    new_latents, error = pl.pallas_call(
        functools.partial(block_kernel, (times, n, heads, rows, width, chan)),
        out_shape=(
            jax.ShapeDtypeStruct((1, chan, rows), wide),
            jax.ShapeDtypeStruct((1,), wide),
        ),
        in_specs=[smem, smem, vmem, vmem, vmem, hbm, hbm, hbm, hbm, hbm],
        out_specs=(vmem, smem),
        scratch_shapes=[
            pltpu.VMEM(w_embed.shape, low),
            pltpu.VMEM(w_mod.shape, low),
            pltpu.VMEM((heads, width, 3 * HD), low),
            pltpu.VMEM(w_out.shape, low),
            pltpu.VMEM((chan, cols), low),
            pltpu.VMEM((rows, chan), low),
            pltpu.VMEM((n, rows, chan), low),
            pltpu.VMEM((5 * n, 1, cols), wide),
            pltpu.VMEM((rows * n, width), wide),
            pltpu.VMEM((rows * n, width), low),
            pltpu.VMEM((n * heads, rows * n, HD), low),
            pltpu.VMEM((rows * n, cols), wide),
            pltpu.VMEM((n - 1, rows + 8, 128), wide),
            pltpu.VMEM((n, rows + 8, 128), wide),
            pltpu.VMEM((times, rows // 2, 128), wide),
            pltpu.VMEM((n, 8, 128), wide),
            dma((4,)),
            dma((heads,)),
            dma((n,)),
            dma((n,)),
            dma((n,)),
            dma((n,)),
            dma((n * heads,)),
            dma((n * heads,)),
            dma((n * heads,)),
            dma((n - 1,)),
            dma((n,)),
            dma((times,)),
            dma((times,)),
            dma((n,)),
            dma((n,)),
        ],
        compiler_params=pltpu.CompilerParams(
            collective_id=0, has_side_effects=True, vmem_limit_bytes=56 * 2**20
        ),
        cost_estimate=pl.CostEstimate(flops=flops, bytes_accessed=16 * 2**20, transcendentals=0),
    )(
        step_index, sigmas, window_start.T, jnp.swapaxes(latents, 1, 2), qk_gain,
        w_embed, w_mod, w_qkv, w_out, w_final.T,
    )
    return jnp.swapaxes(new_latents, 1, 2), error


def fits(times, n, args):
    rows, chan = args[0].shape
    cols = args[4].shape[1] // n
    small = rows * n * args[4].shape[1] <= 384 * 3072
    return times > 2 and n > 1 and cols % 128 == 0 and rows % 32 == 0 and chan == 64 and small


def device_part(*args):
    times, n = lax.axis_size("tm"), lax.axis_size("seq")
    if fits(times, n, args):
        return fused(times, n, *args)
    return shards(*args)


def solution(mesh):
    placed = (
        P("seq", None),
        P("tm", "seq", None),
        P("tm"),
        P(),
        P(),
        P(None, "seq"),
        P(None, "seq"),
        P(None, "seq"),
        P(None, "seq"),
        P("seq", None),
    )
    return jax.shard_map(
        device_part,
        mesh=mesh,
        in_specs=placed,
        out_specs=(P("tm", "seq", None), P("tm")),
        check_vma=False,
    )
```

```python
import functools
import math

import jax
import jax.numpy as jnp
from jax import lax
from jax.experimental import pallas as pl
from jax.experimental.pallas import tpu as pltpu
from jax.sharding import PartitionSpec as P

HD = 128
FREQ = 256


epsilon = 1e-06


def shifted(x, axis, by):
    length = lax.axis_size(axis)
    pairs = [(i, i + by) for i in range(length) if 0 <= i + by < length]
    return lax.ppermute(x, axis, pairs)


def carried_in(part, axis, combine, identity):
    place = lax.axis_index(axis)
    gathered = lax.all_gather(part, axis)
    state = jnp.zeros_like(part) + jnp.asarray(identity, part.dtype)

    def one(lap, state):
        return combine(state, lax.dynamic_index_in_dim(gathered, lap, 0, False))

    return lax.fori_loop(0, place, one, state)


def time_features(moment):
    half_width = FREQ // 2
    frequencies = jnp.exp(
        -math.log(10000.0) * jnp.arange(half_width, dtype=jnp.float32) / half_width
    )
    angles = moment * frequencies
    return jnp.concatenate([jnp.cos(angles), jnp.sin(angles)])


def layer_norm(values):
    average = jnp.mean(values, axis=-1, keepdims=True)
    centered = values - average
    spread = jnp.mean(centered * centered, axis=-1, keepdims=True)
    return centered * lax.rsqrt(spread + epsilon)


def rms_scale(values, gains):
    return values * lax.rsqrt(jnp.mean(values * values, axis=-1, keepdims=True) + epsilon) * gains


def project(state_low, w_embed, modulation, w_qkv, qk_gain):
    row_total = state_low.shape[0]
    block_rows = math.gcd(row_total, 512)
    heads_here = qk_gain.shape[1] // HD
    gains = qk_gain.reshape(2, heads_here, HD)

    def project_one_block(state_block):
        embedded = jnp.dot(state_block, w_embed, preferred_element_type=jnp.float32)
        shaped = (layer_norm(embedded) * (1.0 + modulation[1]) + modulation[0]).astype(jnp.bfloat16)
        mixed = jnp.dot(shaped, w_qkv, preferred_element_type=jnp.float32).reshape(
            block_rows, heads_here, 3, HD
        )
        queries = rms_scale(mixed[:, :, 0], gains[0]).astype(jnp.bfloat16)
        keys_block = rms_scale(mixed[:, :, 1], gains[1]).astype(jnp.bfloat16)
        values_block = mixed[:, :, 2].astype(jnp.bfloat16)
        return (queries, keys_block, values_block)

    blocks = lax.map(
        project_one_block,
        state_low.reshape(row_total // block_rows, block_rows, state_low.shape[1]),
    )
    return tuple((part_block.reshape(row_total, heads_here, HD) for part_block in blocks))


def attend(queries, keys_all, values_all):
    row_total = queries.shape[0]
    heads_here = queries.shape[1]
    block_rows = math.gcd(row_total, 512)

    def attend_one_block(query_block):
        scores = jnp.einsum(
            "qhd,khd->hqk", query_block, keys_all, preferred_element_type=jnp.float32
        ) * HD ** (-0.5)
        highest = jnp.max(scores, axis=-1, keepdims=True)
        raised = jnp.exp(scores - highest)
        weights = (raised / jnp.sum(raised, axis=-1, keepdims=True)).astype(jnp.bfloat16)
        return jnp.einsum(
            "hqk,khd->qhd", weights, values_all, preferred_element_type=jnp.float32
        ).astype(jnp.bfloat16)

    blocks = lax.map(
        attend_one_block, queries.reshape(row_total // block_rows, block_rows, heads_here, HD)
    )
    return blocks.reshape(row_total, heads_here * HD)


def shards(
    window_start, latents, step_index, sigmas, w_embed, w_mod, w_qkv, qk_gain, w_out, w_final
):
    seq_count = lax.axis_size("seq")
    seq_rank = lax.axis_index("seq")
    time_rank = lax.axis_index("tm")
    tok_rows = latents.shape[1]
    all_rows = tok_rows * seq_count
    width = w_embed.shape[1]
    places = jnp.arange(sigmas.shape[0], dtype=jnp.int32)
    sigma_now = jnp.sum(jnp.where(places == step_index[0], sigmas, jnp.zeros_like(sigmas)))
    sigma_next = jnp.sum(jnp.where(places == step_index[0] + 1, sigmas, jnp.zeros_like(sigmas)))
    step_size = sigma_next - sigma_now
    features = time_features(1000.0 * sigma_now).astype(jnp.bfloat16)[None, :]
    mod_piece = jnp.dot(features, w_mod, preferred_element_type=jnp.float32)
    earlier = shifted(latents, "tm", 1)
    state_own = jnp.where(time_rank == 0, window_start, earlier[0])
    state_all, mod_rows = (
        lax.all_gather(state_own, "seq", axis=0, tiled=True),
        lax.all_gather(mod_piece, "seq", axis=0, tiled=True),
    )
    modulation = mod_rows.reshape(5, width)
    state_low = state_all.astype(jnp.bfloat16)
    queries, keys_all, values_all = project(state_low, w_embed, modulation, w_qkv, qk_gain)
    outputs = attend(queries, keys_all, values_all)
    col_count = w_out.shape[1]
    col_first = seq_rank * col_count
    own_heads = lax.all_to_all(outputs, "seq", split_axis=0, concat_axis=1, tiled=True)
    attended = jnp.dot(
        lax.all_gather(own_heads, "seq", axis=0, tiled=True),
        w_out,
        preferred_element_type=jnp.float32,
    )
    embed_cols = jnp.dot(
        state_low,
        lax.dynamic_slice_in_dim(w_embed, col_first, col_count, 1),
        preferred_element_type=jnp.float32,
    )
    mod_cols = lax.dynamic_slice_in_dim(modulation, col_first, col_count, 1)
    hidden = embed_cols + mod_cols[2] * attended
    row_sums, row_squares = lax.psum(
        (jnp.sum(hidden, axis=1), jnp.sum(hidden * hidden, axis=1)), "seq"
    )
    average = row_sums / width
    spread = row_squares / width - average * average
    centered = (hidden - average[:, None]) * lax.rsqrt(spread + epsilon)[:, None]
    normed = (centered * (1.0 + mod_cols[4]) + mod_cols[3]).astype(jnp.bfloat16)
    drift = lax.psum_scatter(
        jnp.dot(normed, w_final, preferred_element_type=jnp.float32).astype(jnp.bfloat16),
        "seq",
        scatter_dimension=0,
        tiled=True,
    ).astype(jnp.float32)
    increment = step_size * drift + jnp.where(
        time_rank == 0, window_start, jnp.zeros_like(window_start)
    )
    increment = increment[None]

    def add_terms(earlier_sum, later_sum):
        return earlier_sum + later_sum

    before = carried_in(increment, "tm", add_terms, jnp.zeros_like(increment))
    new_latents = before + increment
    difference = new_latents - latents
    total_square = lax.psum(jnp.sum(difference * difference), "seq")
    error = (total_square / (all_rows * latents.shape[2])).reshape(1)
    return (new_latents, error)


MESH = pl.DeviceIdType.MESH


def block_kernel(
    dims, index_ref, sigmas_ref, start_hbm, latents_hbm, gains_hbm, w_embed_hbm, w_mod_hbm,
    w_qkv_hbm, w_out_hbm, w_final_hbm, new_hbm, error_ref,
    start_ref, latents_ref, gains_ref, new_ref, w_embed, w_mod, w_qkv, w_out, w_final, state_out, state, mod, embedded, shaped, attended, total,
    part_out, parts, stat_out, stats, sides, terms, squares,
    load_sem, qkv_sem, state_send, state_recv, mod_send, mod_recv, right_send, left_send, att_recv,
    part_send, part_recv, stat_send, stat_recv, side_send, side_recv, term_send, term_recv, square_send, square_recv,
):
    times, n, heads, rows, width, chan = dims
    cols = width // n
    all_rows = rows * n
    me_t, me = lax.axis_index("tm"), lax.axis_index("seq")
    next_t, prev_t = lax.rem(me_t + 1, times), lax.rem(me_t + times - 1, times)

    barrier = pltpu.get_barrier_semaphore()
    peers = []
    for k in range(1, n):
        other = lax.rem(me + k, n)
        peers += [(me_t, other), (next_t, other), (prev_t, other)]
    for k in range(1, times):
        peers.append((lax.rem(me_t + k, times), me))
    for peer in peers:
        pl.semaphore_signal(barrier, inc=1, device_id=peer, device_id_type=MESH)

    load_mod = pltpu.make_async_copy(w_mod_hbm, w_mod, load_sem.at[0])
    load_embed = pltpu.make_async_copy(w_embed_hbm, w_embed, load_sem.at[1])
    load_final = pltpu.make_async_copy(w_final_hbm, w_final, load_sem.at[2])
    load_out = pltpu.make_async_copy(w_out_hbm, w_out, load_sem.at[3])
    small = [
        pltpu.make_async_copy(start_hbm, start_ref, load_sem.at[4]),
        pltpu.make_async_copy(latents_hbm.at[0], latents_ref, load_sem.at[5]),
        pltpu.make_async_copy(gains_hbm, gains_ref, load_sem.at[6]),
    ]
    for load in small:
        load.start()
    load_mod.start()
    load_embed.start()
    for h in range(heads):
        pltpu.make_async_copy(
            w_qkv_hbm.at[:, pl.ds(h * 3 * HD, 3 * HD)], w_qkv.at[h], qkv_sem.at[h]
        ).start()
    load_final.start()
    load_out.start()

    half = rows // 2
    for load in small:
        load.wait()
    own_state = jnp.where(me_t == times - 1, start_ref[...], latents_ref[...]).T
    state_out[...] = jnp.concatenate([own_state[:half], own_state[half:]], axis=1).astype(jnp.bfloat16)

    pl.semaphore_wait(barrier, len(peers))

    def remote(source, target, send, recv, device):
        return pltpu.make_async_remote_copy(
            src_ref=source, dst_ref=target, send_sem=send, recv_sem=recv,
            device_id=device, device_id_type=MESH,
        )

    def state_copy(slot, target):
        return remote(
            state_out, state.at[slot], state_send.at[target], state_recv.at[slot], (next_t, target)
        )

    for k in range(n):
        state_copy(me, k).start()

    def mod_copy(owner, k):
        held = mod.at[pl.ds(owner * 5, 5)]
        return remote(
            held, held, mod_send.at[k], mod_recv.at[owner], (me_t, lax.rem(me + k, n))
        )

    sigma_now = sigmas_ref[index_ref[0]]
    step_size = sigmas_ref[index_ref[0] + 1] - sigma_now
    place = lax.broadcasted_iota(jnp.int32, (16, FREQ // 2), 1).astype(jnp.float32)
    angles = (1000.0 * sigma_now) * jnp.exp(place * (-math.log(10000.0) / (FREQ // 2)))
    features = jnp.concatenate([jnp.cos(angles), jnp.sin(angles)], axis=1).astype(jnp.bfloat16)

    load_mod.wait()
    for i in range(5):
        piece = jnp.dot(
            features, w_mod[:, i * cols : (i + 1) * cols], preferred_element_type=jnp.float32
        )
        mod[me * 5 + i] = piece[0:1]
    for k in range(1, n):
        mod_copy(me, k).start()

    load_embed.wait()
    for k in range(n):
        state_copy(k, 0).wait_recv()
    state_low = jnp.concatenate(
        [state[k // 2, :, (k % 2) * chan : (k % 2 + 1) * chan] for k in range(2 * n)], axis=0
    )
    sums = jnp.zeros((all_rows, 1), jnp.float32)
    for j in range(n):
        tile = jnp.dot(
            state_low, w_embed[:, j * cols : (j + 1) * cols], preferred_element_type=jnp.float32
        )
        embedded[:, j * cols : (j + 1) * cols] = tile
        sums = sums + jnp.sum(tile, axis=1, keepdims=True)
    total[:, 0:1] = sums / width
    for k in range(1, n):
        mod_copy(lax.rem(me + k, n), k).wait_recv()

    block = 32

    def shape_rows(i, carry):
        at = pl.ds(pl.multiple_of(i * block, block), block)
        average = total[at, 0:1]
        spread = jnp.zeros((block, 1), jnp.float32)
        for j in range(n):
            centered = embedded[at, j * cols : (j + 1) * cols] - average
            spread = spread + jnp.sum(centered * centered, axis=1, keepdims=True)
        scale = lax.rsqrt(spread / width + epsilon)
        for j in range(n):
            centered = embedded[at, j * cols : (j + 1) * cols] - average
            value = centered * scale * (1.0 + mod[n + j]) + mod[j]
            shaped[at, j * cols : (j + 1) * cols] = value.astype(jnp.bfloat16)
        return carry

    lax.fori_loop(0, all_rows // block, shape_rows, 0)

    def att_copy(owner, h, right):
        slot = owner * heads + h
        sems = right_send if right else left_send
        held = attended.at[slot]
        return remote(
            held, held, sems.at[slot], att_recv.at[slot], (me_t, me + 1 if right else me - 1)
        )

    def collect(far, h):
        @pl.when(me - far >= 0)
        def _():
            att_copy(me - far, h, True).wait_recv()

            @pl.when(me < n - 1)
            def _():
                att_copy(me - far, h, True).start()

        @pl.when(me + far < n)
        def _():
            att_copy(me + far, h, False).wait_recv()

            @pl.when(me > 0)
            def _():
                att_copy(me + far, h, False).start()

    def one_head(h, carry):
        pltpu.make_async_copy(
            w_qkv_hbm.at[:, pl.ds(0, 3 * HD)], w_qkv.at[h], qkv_sem.at[h]
        ).wait()
        mixed = jnp.dot(shaped[...], w_qkv[h], preferred_element_type=jnp.float32)
        here = pl.ds(pl.multiple_of(h * HD, HD), HD)
        queries = rms_scale(mixed[:, :HD], gains_ref[0:1, here]).astype(jnp.bfloat16)
        keys = rms_scale(mixed[:, HD : 2 * HD], gains_ref[1:2, here]).astype(jnp.bfloat16)
        values = mixed[:, 2 * HD :].astype(jnp.bfloat16)
        scores = lax.dot_general(
            queries, keys, (((1,), (1,)), ((), ())), preferred_element_type=jnp.float32
        )
        raised = jnp.exp((scores - jnp.max(scores, axis=1, keepdims=True)) * HD ** (-0.5))
        weights = raised * (1.0 / jnp.sum(raised, axis=1, keepdims=True))
        attended[me * heads + h] = jnp.dot(
            weights.astype(jnp.bfloat16), values, preferred_element_type=jnp.float32
        ).astype(jnp.bfloat16)

        @pl.when(me < n - 1)
        def _():
            att_copy(me, h, True).start()

        @pl.when(me > 0)
        def _():
            att_copy(me, h, False).start()

        @pl.when(h >= 1)
        def _():
            collect(1, h - 1)

        return carry

    lax.fori_loop(0, heads, one_head, 0)

    load_final.wait()
    load_out.wait()

    def multiply(slot):
        at = pl.ds(pl.multiple_of(slot * HD, HD), HD)
        return jnp.dot(attended[slot], w_out[at, :], preferred_element_type=jnp.float32)

    total[...] = jnp.zeros((all_rows, cols), jnp.float32)

    def own_head(h, carry):
        total[...] += multiply(me * heads + h)
        return carry

    lax.fori_loop(0, heads, own_head, 0)

    gate, shift, scale = mod[2 * n + me], mod[3 * n + me], 1.0 + mod[4 * n + me]
    final = w_final[...]

    def onto_final(x):
        return lax.dot_general(x, final, (((1,), (1,)), ((), ())), preferred_element_type=jnp.float32)

    row = lax.broadcasted_iota(jnp.int32, (16, cols), 0)

    def high(x):
        return x.astype(jnp.bfloat16).astype(jnp.float32)

    stacked = jnp.where(
        row == 0,
        high(scale),
        jnp.where(row == 1, scale - high(scale), jnp.where(row == 2, high(shift), shift - high(shift))),
    )
    row_of = onto_final(stacked.astype(jnp.bfloat16))
    side_row = lax.broadcasted_iota(jnp.int32, (8, chan), 0)
    row_of = jnp.where(
        side_row == 0,
        row_of[0:1] + row_of[1:2],
        jnp.where(side_row == 1, row_of[2:3] + row_of[3:4], 0.0),
    )
    sides[me] = jnp.concatenate([row_of, jnp.zeros((8, 128 - chan), jnp.float32)], axis=1)

    def side_copy(source, k):
        return remote(
            sides.at[source], sides.at[source], side_send.at[k], side_recv.at[source],
            (me_t, lax.rem(me + k, n)),
        )

    for k in range(1, n):
        side_copy(me, k).start()

    def arrived(step, carry):
        far, h = step // heads + 1, lax.rem(step, heads)

        @pl.when((far > 1) | (h == heads - 1))
        def _():
            collect(far, h)

        @pl.when(me - far >= 0)
        def _():
            total[...] += multiply((me - far) * heads + h)

        @pl.when(me + far < n)
        def _():
            total[...] += multiply((me + far) * heads + h)

        return carry

    lax.fori_loop(0, (n - 1) * heads, arrived, 0)

    my_cols = pl.ds(pl.multiple_of(me * cols, cols), cols)
    lane = lax.broadcasted_iota(jnp.int32, (rows, 128 - chan), 1)

    def part_of(owner):
        at = pl.ds(pl.multiple_of(owner * rows, rows), rows)
        hidden = embedded[at, my_cols] + gate * total[at, :]
        middle = jnp.sum(hidden, axis=1, keepdims=True) / cols
        centered = hidden - middle
        square_sums = jnp.sum(centered * centered, axis=1, keepdims=True)
        scaled = centered * scale
        upper = scaled.astype(jnp.bfloat16)
        lower = (scaled - upper.astype(jnp.float32)).astype(jnp.bfloat16)
        product = onto_final(upper) + onto_final(lower)
        own_stats = jnp.where(lane == 0, middle, jnp.where(lane == 1, square_sums, 0.0))
        both = jnp.concatenate([product, own_stats], axis=1).T
        return both[:chan], both[chan : chan + 8]

    def part_copy(k, source, owner):
        return remote(
            part_out.at[k - 1], parts.at[source], part_send.at[k - 1], part_recv.at[source],
            (me_t, owner),
        )

    def stat_copy(k, source, owner):
        return remote(
            stat_out.at[k - 1], stats.at[source], stat_send.at[k - 1], stat_recv.at[source],
            (me_t, owner),
        )

    for k in range(1, n):
        owner = lax.rem(me + k, n)
        product, own_stats = part_of(owner)
        part_out[k - 1] = product.astype(jnp.bfloat16)
        stat_out[k - 1] = own_stats
        part_copy(k, me, owner).start()
        stat_copy(k, me, owner).start()
    products, stats_of, sides_of = [None] * n, [None] * n, [None] * n
    products[0], stats_of[0] = part_of(me)
    sides_of[0] = sides[me].T
    for k in range(1, n):
        source = lax.rem(me + k, n)
        side_copy(source, k).wait_recv()
        sides_of[k] = sides[source].T
    for k in range(1, n):
        source = lax.rem(me + k, n)
        part_copy(k, source, source).wait_recv()
        stat_copy(k, source, source).wait_recv()
        products[k] = parts[source].astype(jnp.float32)
        stats_of[k] = stats[source]
    average = sum(held[0:1] for held in stats_of) / n
    spread = sum(held[1:2] + cols * (held[0:1] - average) ** 2 for held in stats_of) / width
    direct = sum(
        product + side[:chan, 0:1] * (held[0:1] - average)
        for product, side, held in zip(products, sides_of, stats_of)
    )
    drift = direct * lax.rsqrt(spread + epsilon) + sum(side[:chan, 1:2] for side in sides_of)
    increment = step_size * drift
    spare = 128 - rows
    folds = rows // spare
    tail = chan // (folds + 1)
    body = chan - tail
    folded = jnp.concatenate(
        [increment[body:, i * spare : (i + 1) * spare] for i in range(folds)], axis=0
    )
    terms[me_t] = jnp.concatenate([increment[:body], folded], axis=1)

    def term_copy(source, target):
        return remote(
            terms.at[source], terms.at[source], term_send.at[target], term_recv.at[source],
            (target, me),
        )

    for k in range(1, times):

        @pl.when(me_t + k < times)
        def _():
            term_copy(me_t, me_t + k).start()

    for k in range(1, times):

        @pl.when(me_t - k >= 0)
        def _():
            term_copy(me_t - k, me_t).wait_recv()

        @pl.when(me_t - k < 0)
        def _():
            terms[me_t - k + times] = jnp.zeros((body, 128), jnp.float32)

    before = terms[0]
    for k in range(1, times):
        before = before + terms[k]
    unfolded = jnp.concatenate(
        [before[i * tail : (i + 1) * tail, rows:] for i in range(folds)], axis=1
    )
    updated = start_ref[...] + jnp.concatenate([before[:, :rows], unfolded], axis=0)
    new_ref[...] = updated
    store = pltpu.make_async_copy(new_ref, new_hbm.at[0], load_sem.at[7])
    store.start()
    difference = updated - latents_ref[...]
    squares[me] = jnp.broadcast_to(jnp.sum(difference * difference), (8, 128))

    def square_copy(source, k):
        return remote(
            squares.at[source], squares.at[source], square_send.at[k], square_recv.at[source],
            (me_t, lax.rem(me + k, n)),
        )

    for k in range(1, n):
        square_copy(me, k).start()

    for k in range(n):
        state_copy(me, k).wait_send()
    for k in range(1, n):
        mod_copy(me, k).wait_send()
        part_copy(k, me, lax.rem(me + k, n)).wait_send()
        stat_copy(k, me, lax.rem(me + k, n)).wait_send()
        side_copy(me, k).wait_send()
    for k in range(1, times):

        @pl.when(me_t + k < times)
        def _():
            term_copy(me_t, me_t + k).wait_send()

    def all_sent(slot, carry):
        owner, h = slot // heads, lax.rem(slot, heads)

        @pl.when((owner <= me) & (me < n - 1))
        def _():
            att_copy(owner, h, True).wait_send()

        @pl.when((owner >= me) & (me > 0))
        def _():
            att_copy(owner, h, False).wait_send()

        return carry

    lax.fori_loop(0, n * heads, all_sent, 0)
    for k in range(1, n):
        square_copy(me, k).wait_send()
        square_copy(lax.rem(me + k, n), k).wait_recv()
    square_total = squares[0]
    for k in range(1, n):
        square_total = square_total + squares[k]
    store.wait()
    error_ref[0] = jnp.max(square_total) / (all_rows * chan)


def fused(times, n, *args):
    (window_start, latents, step_index, sigmas, w_embed, w_mod, w_qkv, qk_gain, w_out, w_final) = args
    rows, chan = window_start.shape
    width = w_embed.shape[1]
    heads = qk_gain.shape[1] // HD
    cols = width // n
    low, wide = jnp.bfloat16, jnp.float32
    smem, hbm = pl.BlockSpec(memory_space=pltpu.SMEM), pl.BlockSpec(memory_space=pl.ANY)
    dma = pltpu.SemaphoreType.DMA
    flops = 2 * rows * n * (width * heads * 3 * HD + n * heads * HD * cols)
    new_latents, error = pl.pallas_call(
        functools.partial(block_kernel, (times, n, heads, rows, width, chan)),
        out_shape=(
            jax.ShapeDtypeStruct((1, chan, rows), wide),
            jax.ShapeDtypeStruct((1,), wide),
        ),
        in_specs=[smem, smem, hbm, hbm, hbm, hbm, hbm, hbm, hbm, hbm],
        out_specs=(hbm, smem),
        scratch_shapes=[
            pltpu.VMEM((chan, rows), wide),
            pltpu.VMEM((chan, rows), wide),
            pltpu.VMEM(qk_gain.shape, wide),
            pltpu.VMEM((chan, rows), wide),
            pltpu.VMEM(w_embed.shape, low),
            pltpu.VMEM(w_mod.shape, low),
            pltpu.VMEM((heads, width, 3 * HD), low),
            pltpu.VMEM(w_out.shape, low),
            pltpu.VMEM((chan, cols), low),
            pltpu.VMEM((rows // 2, 2 * chan), low),
            pltpu.VMEM((n, rows // 2, 2 * chan), low),
            pltpu.VMEM((5 * n, 1, cols), wide),
            pltpu.VMEM((rows * n, width), wide),
            pltpu.VMEM((rows * n, width), low),
            pltpu.VMEM((n * heads, rows * n, HD), low),
            pltpu.VMEM((rows * n, cols), wide),
            pltpu.VMEM((n - 1, chan, rows), low),
            pltpu.VMEM((n, chan, rows), low),
            pltpu.VMEM((n - 1, 8, rows), wide),
            pltpu.VMEM((n, 8, rows), wide),
            pltpu.VMEM((n, 8, 128), wide),
            pltpu.VMEM((times, chan * rows // 128, 128), wide),
            pltpu.VMEM((n, 8, 128), wide),
            dma((8,)),
            dma((heads,)),
            dma((n,)),
            dma((n,)),
            dma((n,)),
            dma((n,)),
            dma((n * heads,)),
            dma((n * heads,)),
            dma((n * heads,)),
            dma((n - 1,)),
            dma((n,)),
            dma((n - 1,)),
            dma((n,)),
            dma((n,)),
            dma((n,)),
            dma((times,)),
            dma((times,)),
            dma((n,)),
            dma((n,)),
        ],
        compiler_params=pltpu.CompilerParams(
            collective_id=0, has_side_effects=True, vmem_limit_bytes=56 * 2**20
        ),
        cost_estimate=pl.CostEstimate(flops=flops, bytes_accessed=16 * 2**20, transcendentals=0),
    )(
        step_index, sigmas, window_start.T, jnp.swapaxes(latents, 1, 2), qk_gain,
        w_embed, w_mod, w_qkv, w_out, w_final.T,
    )
    return jnp.swapaxes(new_latents, 1, 2), error


def fits(times, n, args):
    rows, chan = args[0].shape
    cols = args[4].shape[1] // n
    small = rows * n * args[4].shape[1] <= 384 * 3072
    return times > 2 and n > 1 and cols % 128 == 0 and rows in (64, 96) and chan == 64 and small


def device_part(*args):
    times, n = lax.axis_size("tm"), lax.axis_size("seq")
    if fits(times, n, args):
        return fused(times, n, *args)
    return shards(*args)


def solution(mesh):
    placed = (
        P("seq", None),
        P("tm", "seq", None),
        P("tm"),
        P(),
        P(),
        P(None, "seq"),
        P(None, "seq"),
        P(None, "seq"),
        P(None, "seq"),
        P("seq", None),
    )
    return jax.shard_map(
        device_part,
        mesh=mesh,
        in_specs=placed,
        out_specs=(P("tm", "seq", None), P("tm")),
        check_vma=False,
    )
```

```python
import functools
import math

import jax
import jax.numpy as jnp
from jax import lax
from jax.experimental import pallas as pl
from jax.experimental.pallas import tpu as pltpu
from jax.sharding import PartitionSpec as P

HD = 128
FREQ = 256


epsilon = 1e-06


def shifted(x, axis, by):
    length = lax.axis_size(axis)
    pairs = [(i, i + by) for i in range(length) if 0 <= i + by < length]
    return lax.ppermute(x, axis, pairs)


def carried_in(part, axis, combine, identity):
    place = lax.axis_index(axis)
    gathered = lax.all_gather(part, axis)
    state = jnp.zeros_like(part) + jnp.asarray(identity, part.dtype)

    def one(lap, state):
        return combine(state, lax.dynamic_index_in_dim(gathered, lap, 0, False))

    return lax.fori_loop(0, place, one, state)


def time_features(moment):
    half_width = FREQ // 2
    frequencies = jnp.exp(
        -math.log(10000.0) * jnp.arange(half_width, dtype=jnp.float32) / half_width
    )
    angles = moment * frequencies
    return jnp.concatenate([jnp.cos(angles), jnp.sin(angles)])


def layer_norm(values):
    average = jnp.mean(values, axis=-1, keepdims=True)
    centered = values - average
    spread = jnp.mean(centered * centered, axis=-1, keepdims=True)
    return centered * lax.rsqrt(spread + epsilon)


def rms_scale(values, gains):
    return values * lax.rsqrt(jnp.mean(values * values, axis=-1, keepdims=True) + epsilon) * gains


def project(state_low, w_embed, modulation, w_qkv, qk_gain):
    row_total = state_low.shape[0]
    block_rows = math.gcd(row_total, 512)
    heads_here = qk_gain.shape[1] // HD
    gains = qk_gain.reshape(2, heads_here, HD)

    def project_one_block(state_block):
        embedded = jnp.dot(state_block, w_embed, preferred_element_type=jnp.float32)
        shaped = (layer_norm(embedded) * (1.0 + modulation[1]) + modulation[0]).astype(jnp.bfloat16)
        mixed = jnp.dot(shaped, w_qkv, preferred_element_type=jnp.float32).reshape(
            block_rows, heads_here, 3, HD
        )
        queries = rms_scale(mixed[:, :, 0], gains[0]).astype(jnp.bfloat16)
        keys_block = rms_scale(mixed[:, :, 1], gains[1]).astype(jnp.bfloat16)
        values_block = mixed[:, :, 2].astype(jnp.bfloat16)
        return (queries, keys_block, values_block)

    blocks = lax.map(
        project_one_block,
        state_low.reshape(row_total // block_rows, block_rows, state_low.shape[1]),
    )
    return tuple((part_block.reshape(row_total, heads_here, HD) for part_block in blocks))


def attend(queries, keys_all, values_all):
    row_total = queries.shape[0]
    heads_here = queries.shape[1]
    block_rows = math.gcd(row_total, 512)

    def attend_one_block(query_block):
        scores = jnp.einsum(
            "qhd,khd->hqk", query_block, keys_all, preferred_element_type=jnp.float32
        ) * HD ** (-0.5)
        highest = jnp.max(scores, axis=-1, keepdims=True)
        raised = jnp.exp(scores - highest)
        weights = (raised / jnp.sum(raised, axis=-1, keepdims=True)).astype(jnp.bfloat16)
        return jnp.einsum(
            "hqk,khd->qhd", weights, values_all, preferred_element_type=jnp.float32
        ).astype(jnp.bfloat16)

    blocks = lax.map(
        attend_one_block, queries.reshape(row_total // block_rows, block_rows, heads_here, HD)
    )
    return blocks.reshape(row_total, heads_here * HD)


def shards(
    window_start, latents, step_index, sigmas, w_embed, w_mod, w_qkv, qk_gain, w_out, w_final
):
    seq_count = lax.axis_size("seq")
    seq_rank = lax.axis_index("seq")
    time_rank = lax.axis_index("tm")
    tok_rows = latents.shape[1]
    all_rows = tok_rows * seq_count
    width = w_embed.shape[1]
    places = jnp.arange(sigmas.shape[0], dtype=jnp.int32)
    sigma_now = jnp.sum(jnp.where(places == step_index[0], sigmas, jnp.zeros_like(sigmas)))
    sigma_next = jnp.sum(jnp.where(places == step_index[0] + 1, sigmas, jnp.zeros_like(sigmas)))
    step_size = sigma_next - sigma_now
    features = time_features(1000.0 * sigma_now).astype(jnp.bfloat16)[None, :]
    mod_piece = jnp.dot(features, w_mod, preferred_element_type=jnp.float32)
    earlier = shifted(latents, "tm", 1)
    state_own = jnp.where(time_rank == 0, window_start, earlier[0])
    state_all, mod_rows = (
        lax.all_gather(state_own, "seq", axis=0, tiled=True),
        lax.all_gather(mod_piece, "seq", axis=0, tiled=True),
    )
    modulation = mod_rows.reshape(5, width)
    state_low = state_all.astype(jnp.bfloat16)
    queries, keys_all, values_all = project(state_low, w_embed, modulation, w_qkv, qk_gain)
    outputs = attend(queries, keys_all, values_all)
    col_count = w_out.shape[1]
    col_first = seq_rank * col_count
    own_heads = lax.all_to_all(outputs, "seq", split_axis=0, concat_axis=1, tiled=True)
    attended = jnp.dot(
        lax.all_gather(own_heads, "seq", axis=0, tiled=True),
        w_out,
        preferred_element_type=jnp.float32,
    )
    embed_cols = jnp.dot(
        state_low,
        lax.dynamic_slice_in_dim(w_embed, col_first, col_count, 1),
        preferred_element_type=jnp.float32,
    )
    mod_cols = lax.dynamic_slice_in_dim(modulation, col_first, col_count, 1)
    hidden = embed_cols + mod_cols[2] * attended
    row_sums, row_squares = lax.psum(
        (jnp.sum(hidden, axis=1), jnp.sum(hidden * hidden, axis=1)), "seq"
    )
    average = row_sums / width
    spread = row_squares / width - average * average
    centered = (hidden - average[:, None]) * lax.rsqrt(spread + epsilon)[:, None]
    normed = (centered * (1.0 + mod_cols[4]) + mod_cols[3]).astype(jnp.bfloat16)
    drift = lax.psum_scatter(
        jnp.dot(normed, w_final, preferred_element_type=jnp.float32).astype(jnp.bfloat16),
        "seq",
        scatter_dimension=0,
        tiled=True,
    ).astype(jnp.float32)
    increment = step_size * drift + jnp.where(
        time_rank == 0, window_start, jnp.zeros_like(window_start)
    )
    increment = increment[None]

    def add_terms(earlier_sum, later_sum):
        return earlier_sum + later_sum

    before = carried_in(increment, "tm", add_terms, jnp.zeros_like(increment))
    new_latents = before + increment
    difference = new_latents - latents
    total_square = lax.psum(jnp.sum(difference * difference), "seq")
    error = (total_square / (all_rows * latents.shape[2])).reshape(1)
    return (new_latents, error)


MESH = pl.DeviceIdType.MESH


def block_kernel(
    dims, index_ref, sigmas_ref, start_hbm, latents_hbm, gains_hbm, w_embed_hbm, w_mod_hbm,
    w_qkv_hbm, w_out_hbm, w_final_hbm, new_hbm, error_ref,
    start_ref, latents_ref, gains_ref, new_ref, w_embed, w_mod, w_qkv, w_out, w_final, state_out, state, mod, embedded, shaped, attended, total,
    part_out, parts, stat_out, stats, sides, terms, squares,
    load_sem, qkv_sem, state_send, state_recv, mod_send, mod_recv, right_send, left_send, att_recv,
    part_send, part_recv, stat_send, stat_recv, side_send, side_recv, term_send, term_recv, square_send, square_recv,
):
    times, n, heads, rows, width, chan = dims
    cols = width // n
    all_rows = rows * n
    me_t, me = lax.axis_index("tm"), lax.axis_index("seq")
    next_t, prev_t = lax.rem(me_t + 1, times), lax.rem(me_t + times - 1, times)

    barrier = pltpu.get_barrier_semaphore()
    peers = []
    for k in range(1, n):
        other = lax.rem(me + k, n)
        peers += [(me_t, other), (next_t, other), (prev_t, other)]
    for k in range(1, times):
        peers.append((lax.rem(me_t + k, times), me))
    for peer in peers:
        pl.semaphore_signal(barrier, inc=1, device_id=peer, device_id_type=MESH)

    load_mod = pltpu.make_async_copy(w_mod_hbm, w_mod, load_sem.at[0])
    load_embed = pltpu.make_async_copy(w_embed_hbm, w_embed, load_sem.at[1])
    load_final = pltpu.make_async_copy(w_final_hbm, w_final, load_sem.at[2])
    load_out = pltpu.make_async_copy(w_out_hbm, w_out, load_sem.at[3])
    small = [
        pltpu.make_async_copy(start_hbm, start_ref, load_sem.at[4]),
        pltpu.make_async_copy(latents_hbm.at[0], latents_ref, load_sem.at[5]),
        pltpu.make_async_copy(gains_hbm, gains_ref, load_sem.at[6]),
    ]
    for load in small:
        load.start()
    load_mod.start()
    load_embed.start()
    for h in range(heads):
        pltpu.make_async_copy(
            w_qkv_hbm.at[:, pl.ds(h * 3 * HD, 3 * HD)], w_qkv.at[h], qkv_sem.at[h]
        ).start()
    load_final.start()
    load_out.start()

    half = rows // 2
    for load in small:
        load.wait()
    own_state = jnp.where(me_t == times - 1, start_ref[...], latents_ref[...]).T
    state_out[...] = jnp.concatenate([own_state[:half], own_state[half:]], axis=1).astype(jnp.bfloat16)

    def remote(source, target, send, recv, device):
        return pltpu.make_async_remote_copy(
            src_ref=source, dst_ref=target, send_sem=send, recv_sem=recv,
            device_id=device, device_id_type=MESH,
        )

    def state_copy(slot, target):
        return remote(
            state_out, state.at[slot], state_send.at[target], state_recv.at[slot], (next_t, target)
        )


    def mod_copy(owner, k):
        held = mod.at[pl.ds(owner * 5, 5)]
        return remote(
            held, held, mod_send.at[k], mod_recv.at[owner], (me_t, lax.rem(me + k, n))
        )

    sigma_now = sigmas_ref[index_ref[0]]
    step_size = sigmas_ref[index_ref[0] + 1] - sigma_now
    place = lax.broadcasted_iota(jnp.int32, (16, FREQ // 2), 1).astype(jnp.float32)
    angles = (1000.0 * sigma_now) * jnp.exp(place * (-math.log(10000.0) / (FREQ // 2)))
    features = jnp.concatenate([jnp.cos(angles), jnp.sin(angles)], axis=1).astype(jnp.bfloat16)

    load_mod.wait()
    for i in range(5):
        piece = jnp.dot(
            features, w_mod[:, i * cols : (i + 1) * cols], preferred_element_type=jnp.float32
        )
        mod[me * 5 + i] = piece[0:1]
    pl.semaphore_wait(barrier, len(peers))
    for k in range(n):
        state_copy(me, k).start()
    for k in range(1, n):
        mod_copy(me, k).start()

    load_embed.wait()
    for k in range(n):
        state_copy(k, 0).wait_recv()
    state_low = jnp.concatenate(
        [state[k // 2, :, (k % 2) * chan : (k % 2 + 1) * chan] for k in range(2 * n)], axis=0
    )
    sums = jnp.zeros((all_rows, 1), jnp.float32)
    for j in range(n):
        tile = jnp.dot(
            state_low, w_embed[:, j * cols : (j + 1) * cols], preferred_element_type=jnp.float32
        )
        embedded[:, j * cols : (j + 1) * cols] = tile
        sums = sums + jnp.sum(tile, axis=1, keepdims=True)
    total[:, 0:1] = sums / width
    for k in range(1, n):
        mod_copy(lax.rem(me + k, n), k).wait_recv()

    block = 32

    def shape_rows(i, carry):
        at = pl.ds(pl.multiple_of(i * block, block), block)
        average = total[at, 0:1]
        spread = jnp.zeros((block, 1), jnp.float32)
        for j in range(n):
            centered = embedded[at, j * cols : (j + 1) * cols] - average
            spread = spread + jnp.sum(centered * centered, axis=1, keepdims=True)
        scale = lax.rsqrt(spread / width + epsilon)
        for j in range(n):
            centered = embedded[at, j * cols : (j + 1) * cols] - average
            value = centered * scale * (1.0 + mod[n + j]) + mod[j]
            shaped[at, j * cols : (j + 1) * cols] = value.astype(jnp.bfloat16)
        return carry

    lax.fori_loop(0, all_rows // block, shape_rows, 0)

    def att_copy(owner, h, right):
        slot = owner * heads + h
        sems = right_send if right else left_send
        held = attended.at[slot]
        return remote(
            held, held, sems.at[slot], att_recv.at[slot], (me_t, me + 1 if right else me - 1)
        )

    def collect(far, h):
        @pl.when(me - far >= 0)
        def _():
            att_copy(me - far, h, True).wait_recv()

            @pl.when(me < n - 1)
            def _():
                att_copy(me - far, h, True).start()

        @pl.when(me + far < n)
        def _():
            att_copy(me + far, h, False).wait_recv()

            @pl.when(me > 0)
            def _():
                att_copy(me + far, h, False).start()

    def one_head(h, carry):
        pltpu.make_async_copy(
            w_qkv_hbm.at[:, pl.ds(0, 3 * HD)], w_qkv.at[h], qkv_sem.at[h]
        ).wait()
        mixed = jnp.dot(shaped[...], w_qkv[h], preferred_element_type=jnp.float32)
        here = pl.ds(pl.multiple_of(h * HD, HD), HD)
        queries = rms_scale(mixed[:, :HD], gains_ref[0:1, here]).astype(jnp.bfloat16)
        keys = rms_scale(mixed[:, HD : 2 * HD], gains_ref[1:2, here]).astype(jnp.bfloat16)
        values = mixed[:, 2 * HD :].astype(jnp.bfloat16)
        scores = lax.dot_general(
            queries, keys, (((1,), (1,)), ((), ())), preferred_element_type=jnp.float32
        )
        raised = jnp.exp((scores - jnp.max(scores, axis=1, keepdims=True)) * HD ** (-0.5))
        weights = raised * (1.0 / jnp.sum(raised, axis=1, keepdims=True))
        attended[me * heads + h] = jnp.dot(
            weights.astype(jnp.bfloat16), values, preferred_element_type=jnp.float32
        ).astype(jnp.bfloat16)

        @pl.when(me < n - 1)
        def _():
            att_copy(me, h, True).start()

        @pl.when(me > 0)
        def _():
            att_copy(me, h, False).start()

        @pl.when(h >= 1)
        def _():
            collect(1, h - 1)

        return carry

    lax.fori_loop(0, heads, one_head, 0)

    load_final.wait()
    load_out.wait()

    def multiply(slot):
        at = pl.ds(pl.multiple_of(slot * HD, HD), HD)
        return jnp.dot(attended[slot], w_out[at, :], preferred_element_type=jnp.float32)

    total[...] = jnp.zeros((all_rows, cols), jnp.float32)

    def own_head(h, carry):
        total[...] += multiply(me * heads + h)
        return carry

    lax.fori_loop(0, heads, own_head, 0)

    gate, shift, scale = mod[2 * n + me], mod[3 * n + me], 1.0 + mod[4 * n + me]
    final = w_final[...]

    def onto_final(x):
        return lax.dot_general(x, final, (((1,), (1,)), ((), ())), preferred_element_type=jnp.float32)

    row = lax.broadcasted_iota(jnp.int32, (16, cols), 0)

    def high(x):
        return x.astype(jnp.bfloat16).astype(jnp.float32)

    stacked = jnp.where(
        row == 0,
        high(scale),
        jnp.where(row == 1, scale - high(scale), jnp.where(row == 2, high(shift), shift - high(shift))),
    )
    row_of = onto_final(stacked.astype(jnp.bfloat16))
    side_row = lax.broadcasted_iota(jnp.int32, (8, chan), 0)
    row_of = jnp.where(
        side_row == 0,
        row_of[0:1] + row_of[1:2],
        jnp.where(side_row == 1, row_of[2:3] + row_of[3:4], 0.0),
    )
    sides[me] = jnp.concatenate([row_of, jnp.zeros((8, 128 - chan), jnp.float32)], axis=1)

    def side_copy(source, k):
        return remote(
            sides.at[source], sides.at[source], side_send.at[k], side_recv.at[source],
            (me_t, lax.rem(me + k, n)),
        )

    for k in range(1, n):
        side_copy(me, k).start()

    def arrived(step, carry):
        far, h = step // heads + 1, lax.rem(step, heads)

        @pl.when((far > 1) | (h == heads - 1))
        def _():
            collect(far, h)

        @pl.when(me - far >= 0)
        def _():
            total[...] += multiply((me - far) * heads + h)

        @pl.when(me + far < n)
        def _():
            total[...] += multiply((me + far) * heads + h)

        return carry

    lax.fori_loop(0, (n - 1) * heads, arrived, 0)

    my_cols = pl.ds(pl.multiple_of(me * cols, cols), cols)
    lane = lax.broadcasted_iota(jnp.int32, (rows, 128 - chan), 1)

    def part_of(owner):
        at = pl.ds(pl.multiple_of(owner * rows, rows), rows)
        hidden = embedded[at, my_cols] + gate * total[at, :]
        middle = jnp.sum(hidden, axis=1, keepdims=True) / cols
        centered = hidden - middle
        square_sums = jnp.sum(centered * centered, axis=1, keepdims=True)
        scaled = centered * scale
        upper = scaled.astype(jnp.bfloat16)
        lower = (scaled - upper.astype(jnp.float32)).astype(jnp.bfloat16)
        product = onto_final(upper) + onto_final(lower)
        own_stats = jnp.where(lane == 0, middle, jnp.where(lane == 1, square_sums, 0.0))
        both = jnp.concatenate([product, own_stats], axis=1).T
        return both[:chan], both[chan : chan + 8]

    def part_copy(k, source, owner):
        return remote(
            part_out.at[k - 1], parts.at[source], part_send.at[k - 1], part_recv.at[source],
            (me_t, owner),
        )

    def stat_copy(k, source, owner):
        return remote(
            stat_out.at[k - 1], stats.at[source], stat_send.at[k - 1], stat_recv.at[source],
            (me_t, owner),
        )

    for k in range(1, n):
        owner = lax.rem(me + k, n)
        product, own_stats = part_of(owner)
        part_out[k - 1] = product.astype(jnp.bfloat16)
        stat_out[k - 1] = own_stats
        part_copy(k, me, owner).start()
        stat_copy(k, me, owner).start()
    products, stats_of, sides_of = [None] * n, [None] * n, [None] * n
    products[0], stats_of[0] = part_of(me)
    sides_of[0] = sides[me].T
    for k in range(1, n):
        source = lax.rem(me + k, n)
        side_copy(source, k).wait_recv()
        sides_of[k] = sides[source].T
    for k in range(1, n):
        source = lax.rem(me + k, n)
        part_copy(k, source, source).wait_recv()
        stat_copy(k, source, source).wait_recv()
        products[k] = parts[source].astype(jnp.float32)
        stats_of[k] = stats[source]
    average = sum(held[0:1] for held in stats_of) / n
    spread = sum(held[1:2] + cols * (held[0:1] - average) ** 2 for held in stats_of) / width
    direct = sum(
        product + side[:chan, 0:1] * (held[0:1] - average)
        for product, side, held in zip(products, sides_of, stats_of)
    )
    drift = direct * lax.rsqrt(spread + epsilon) + sum(side[:chan, 1:2] for side in sides_of)
    increment = step_size * drift
    spare = 128 - rows
    folds = rows // spare
    tail = chan // (folds + 1)
    body = chan - tail
    folded = jnp.concatenate(
        [increment[body:, i * spare : (i + 1) * spare] for i in range(folds)], axis=0
    )
    terms[me_t] = jnp.concatenate([increment[:body], folded], axis=1)

    def term_copy(source, target):
        return remote(
            terms.at[source], terms.at[source], term_send.at[target], term_recv.at[source],
            (target, me),
        )

    for k in range(1, times):

        @pl.when(me_t + k < times)
        def _():
            term_copy(me_t, me_t + k).start()

    for k in range(1, times):

        @pl.when(me_t - k >= 0)
        def _():
            term_copy(me_t - k, me_t).wait_recv()

        @pl.when(me_t - k < 0)
        def _():
            terms[me_t - k + times] = jnp.zeros((body, 128), jnp.float32)

    before = terms[0]
    for k in range(1, times):
        before = before + terms[k]
    unfolded = jnp.concatenate(
        [before[i * tail : (i + 1) * tail, rows:] for i in range(folds)], axis=1
    )
    updated = start_ref[...] + jnp.concatenate([before[:, :rows], unfolded], axis=0)
    new_ref[...] = updated
    store = pltpu.make_async_copy(new_ref, new_hbm.at[0], load_sem.at[7])
    store.start()
    difference = updated - latents_ref[...]
    squares[me] = jnp.broadcast_to(jnp.sum(difference * difference), (8, 128))

    def square_copy(source, k):
        return remote(
            squares.at[source], squares.at[source], square_send.at[k], square_recv.at[source],
            (me_t, lax.rem(me + k, n)),
        )

    for k in range(1, n):
        square_copy(me, k).start()

    for k in range(n):
        state_copy(me, k).wait_send()
    for k in range(1, n):
        mod_copy(me, k).wait_send()
        part_copy(k, me, lax.rem(me + k, n)).wait_send()
        stat_copy(k, me, lax.rem(me + k, n)).wait_send()
        side_copy(me, k).wait_send()
    for k in range(1, times):

        @pl.when(me_t + k < times)
        def _():
            term_copy(me_t, me_t + k).wait_send()

    def all_sent(slot, carry):
        owner, h = slot // heads, lax.rem(slot, heads)

        @pl.when((owner <= me) & (me < n - 1))
        def _():
            att_copy(owner, h, True).wait_send()

        @pl.when((owner >= me) & (me > 0))
        def _():
            att_copy(owner, h, False).wait_send()

        return carry

    lax.fori_loop(0, n * heads, all_sent, 0)
    for k in range(1, n):
        square_copy(me, k).wait_send()
        square_copy(lax.rem(me + k, n), k).wait_recv()
    square_total = squares[0]
    for k in range(1, n):
        square_total = square_total + squares[k]
    store.wait()
    error_ref[0] = jnp.max(square_total) / (all_rows * chan)


def fused(times, n, *args):
    (window_start, latents, step_index, sigmas, w_embed, w_mod, w_qkv, qk_gain, w_out, w_final) = args
    rows, chan = window_start.shape
    width = w_embed.shape[1]
    heads = qk_gain.shape[1] // HD
    cols = width // n
    low, wide = jnp.bfloat16, jnp.float32
    smem, hbm = pl.BlockSpec(memory_space=pltpu.SMEM), pl.BlockSpec(memory_space=pl.ANY)
    dma = pltpu.SemaphoreType.DMA
    flops = 2 * rows * n * (width * heads * 3 * HD + n * heads * HD * cols)
    new_latents, error = pl.pallas_call(
        functools.partial(block_kernel, (times, n, heads, rows, width, chan)),
        out_shape=(
            jax.ShapeDtypeStruct((1, chan, rows), wide),
            jax.ShapeDtypeStruct((1,), wide),
        ),
        in_specs=[smem, smem, hbm, hbm, hbm, hbm, hbm, hbm, hbm, hbm],
        out_specs=(hbm, smem),
        scratch_shapes=[
            pltpu.VMEM((chan, rows), wide),
            pltpu.VMEM((chan, rows), wide),
            pltpu.VMEM(qk_gain.shape, wide),
            pltpu.VMEM((chan, rows), wide),
            pltpu.VMEM(w_embed.shape, low),
            pltpu.VMEM(w_mod.shape, low),
            pltpu.VMEM((heads, width, 3 * HD), low),
            pltpu.VMEM(w_out.shape, low),
            pltpu.VMEM((chan, cols), low),
            pltpu.VMEM((rows // 2, 2 * chan), low),
            pltpu.VMEM((n, rows // 2, 2 * chan), low),
            pltpu.VMEM((5 * n, 1, cols), wide),
            pltpu.VMEM((rows * n, width), wide),
            pltpu.VMEM((rows * n, width), low),
            pltpu.VMEM((n * heads, rows * n, HD), low),
            pltpu.VMEM((rows * n, cols), wide),
            pltpu.VMEM((n - 1, chan, rows), low),
            pltpu.VMEM((n, chan, rows), low),
            pltpu.VMEM((n - 1, 8, rows), wide),
            pltpu.VMEM((n, 8, rows), wide),
            pltpu.VMEM((n, 8, 128), wide),
            pltpu.VMEM((times, chan * rows // 128, 128), wide),
            pltpu.VMEM((n, 8, 128), wide),
            dma((8,)),
            dma((heads,)),
            dma((n,)),
            dma((n,)),
            dma((n,)),
            dma((n,)),
            dma((n * heads,)),
            dma((n * heads,)),
            dma((n * heads,)),
            dma((n - 1,)),
            dma((n,)),
            dma((n - 1,)),
            dma((n,)),
            dma((n,)),
            dma((n,)),
            dma((times,)),
            dma((times,)),
            dma((n,)),
            dma((n,)),
        ],
        compiler_params=pltpu.CompilerParams(
            collective_id=0, has_side_effects=True, vmem_limit_bytes=56 * 2**20
        ),
        cost_estimate=pl.CostEstimate(flops=flops, bytes_accessed=16 * 2**20, transcendentals=0),
    )(
        step_index, sigmas, window_start.T, jnp.swapaxes(latents, 1, 2), qk_gain,
        w_embed, w_mod, w_qkv, w_out, w_final.T,
    )
    return jnp.swapaxes(new_latents, 1, 2), error


def fits(times, n, args):
    rows, chan = args[0].shape
    cols = args[4].shape[1] // n
    small = rows * n * args[4].shape[1] <= 384 * 3072
    return times > 2 and n > 1 and cols % 128 == 0 and rows in (64, 96) and chan == 64 and small


def device_part(*args):
    times, n = lax.axis_size("tm"), lax.axis_size("seq")
    if fits(times, n, args):
        return fused(times, n, *args)
    return shards(*args)


def solution(mesh):
    placed = (
        P("seq", None),
        P("tm", "seq", None),
        P("tm"),
        P(),
        P(),
        P(None, "seq"),
        P(None, "seq"),
        P(None, "seq"),
        P(None, "seq"),
        P("seq", None),
    )
    return jax.shard_map(
        device_part,
        mesh=mesh,
        in_specs=placed,
        out_specs=(P("tm", "seq", None), P("tm")),
        check_vma=False,
    )
```
